128 devices in a mesh: views: 16 (over x, y), sub: 8 (over z, core).
Axes of the slice: x: 4, y: 4, z: 4, core: 2. Of those that a mesh axis runs over, the one named last changes fastest.
Arguments:
- queries: bfloat16 [32768, 512], P(('views', 'sub')), may hold values from -300 to 300
- keys: bfloat16 [32768, 512], P(('views', 'sub')), may hold values from -7 to 7
- values: bfloat16 [32768, 512], P(('views', 'sub')), may hold values from -6 to 6
- out_grad: bfloat16 [32768, 512], P(('views', 'sub')), may hold values from -6 to 6
- block_lists: int32 [256, 16], P(('views', 'sub')), may hold values from -1 to 255, as said below
Outputs:
- query_grad: bfloat16 [32768, 512], P(('views', 'sub'))
- key_grad: bfloat16 [32768, 512], P(('views', 'sub'))
- value_grad: bfloat16 [32768, 512], P(('views', 'sub'))
The draws below stay inside these ranges and needn't reach their ends.
Inputs may be any that keep to these rules, and one draw needn't show every extreme that they name: `block_lists`: an entry is -1 (no block) or the number of a key block of another view that lies at the same band position, sub index, as the query block; the entries of one query block are distinct. Of all entries of the 2 query blocks of one band of one view, at most 1 name blocks of any one view, and exactly 1 name blocks of some view.
All inputs are finite; a program needn't handle non-finite values.
Results may differ from the reference program's by a relative error of at most 0.0075.
Values may be sent and summed in bfloat16 or wider, within the bound.
A program may use at most 192 MiB of HBM per device.

```python
import jax
import jax.numpy as jnp
from jax import lax

D = 512
HEADS = 8
BLOCK = 128
NBLK = 2
LIST = 16
CAP = 1
TOKENS = 32768
N_VIEWS = 16
N_SUB = 8


def shared_normal(key):
    return jnp.clip(jax.random.normal(key, (TOKENS, D), jnp.float32), -6.0, 6.0)


def draw_keys(key, part):
    normal_base = shared_normal(key)
    return normal_base.astype(jnp.bfloat16)


def draw_queries(key, part):
    key = jax.random.fold_in(key, 5)
    fresh = jnp.clip(jax.random.normal(key, (TOKENS, D), jnp.float32), -6.0, 6.0)
    return fresh.astype(jnp.bfloat16)


def draw_block_lists(key, part):
    key = jax.random.fold_in(key, 7)
    device_count = N_VIEWS * N_SUB
    pair_count = NBLK * NBLK
    key_counts, key_forced, key_pairs, key_slots = jax.random.split(key, 4)
    device_ids = jnp.arange(device_count)
    own_view = device_ids // N_SUB
    band_ids = device_ids % N_SUB
    views_iota = jnp.arange(N_VIEWS)
    counts = jax.random.randint(key_counts, (device_count, N_VIEWS), 0, CAP + 1)
    offset_view = jax.random.randint(key_forced, (device_count,), 1, N_VIEWS)
    forced = (own_view + offset_view) % N_VIEWS
    counts = jnp.where(views_iota[None, :] == forced[:, None], CAP, counts)
    counts = jnp.where(views_iota[None, :] == own_view[:, None], 0, counts)
    scores = jax.random.randint(key_pairs, (device_count, N_VIEWS, pair_count), 0, 1 << 20) * pair_count + jnp.arange(pair_count)
    ordering = jnp.argsort(scores, axis=-1)
    pair_rank = jnp.argsort(ordering, axis=-1)
    chosen = (pair_rank < counts[:, :, None]).reshape(device_count, N_VIEWS, NBLK, NBLK)
    local_ids = jnp.arange(NBLK)
    block_ids = views_iota[None, :, None, None] * (N_SUB * NBLK) + band_ids[:, None, None, None] * NBLK + local_ids[None, None, None, :]
    candidate = jnp.where(chosen, block_ids, -1)
    candidate = jnp.transpose(candidate, (0, 2, 1, 3)).reshape(device_count, NBLK, N_VIEWS * NBLK)
    is_live = candidate >= 0
    live_rank = jnp.cumsum(is_live.astype(jnp.int32), axis=-1) - 1
    live_rank = jnp.clip(live_rank, 0, LIST - 1)
    slot_scores = jax.random.randint(key_slots, (device_count, NBLK, LIST), 0, 1 << 20) * LIST + jnp.arange(LIST)
    slot_perm = jnp.argsort(slot_scores, axis=-1)
    target = jnp.take_along_axis(slot_perm, live_rank, axis=-1)
    placed = is_live[:, :, :, None] & (target[:, :, :, None] == jnp.arange(LIST)[None, None, None, :])
    block_table = jnp.sum(jnp.where(placed, candidate[:, :, :, None] + 1, 0), axis=2) - 1
    return block_table.reshape(device_count * NBLK, LIST).astype(jnp.int32)


def block_scale(own_key, extent, cuts, smallest, high):
    gain, own = 1.0, jax.random.fold_in(own_key, 6)
    for dim, blocks in cuts:
        heights = jnp.exp(jax.random.uniform(jax.random.fold_in(own, dim), (blocks,), jnp.float32, smallest / len(cuts), high / len(cuts)))
        gain = gain * jnp.repeat(heights, extent[dim] // blocks).reshape([-1 if axis == dim else 1 for axis in range(len(extent))])
    return gain


def bell_draw(stream_key, extent, spread, most, pieces=(), kind=jnp.bfloat16):
    level = block_scale(stream_key, extent, pieces, -0.22, 0.18) if pieces else 1.0
    entries = jax.random.normal(stream_key, extent, jnp.float32) * spread * level
    return jnp.minimum(jnp.maximum(entries, -most), most).astype(kind)


def setup_inputs(seed: int = 0) -> dict:
    splits = jax.random.split(jax.random.key(seed), 6)
    queries = draw_queries(jax.random.fold_in(splits[5], 71), 0)
    keys = draw_keys(jax.random.fold_in(splits[5], 71), 0)
    values = bell_draw(splits[2], (TOKENS, D), 1.0, 6.0, ((0, 128),))
    out_grad = bell_draw(splits[3], (TOKENS, D), 1.0, 6.0, ((0, 128),))
    block_lists = draw_block_lists(jax.random.fold_in(splits[5], 71), 0)
    return {"queries": queries, "keys": keys, "values": values, "out_grad": out_grad, "block_lists": block_lists}


masked_score = -1.0e30


def block_backward(query_blk, grad_blk, key_set, value_set, usable):
    head_size = query_blk.shape[-1]
    scaling = head_size ** -0.5
    query_f = query_blk.astype(jnp.float32)
    grad_f = grad_blk.astype(jnp.float32)
    key_f = key_set.astype(jnp.float32)
    value_f = value_set.astype(jnp.float32)
    scores = jnp.einsum('ihd,kjhd->hikj', query_f, key_f) * scaling
    scores = jnp.where(usable[None, None, :, None], scores, masked_score)
    row_max = jnp.max(scores, axis=(2, 3), keepdims=True)
    raised = jnp.exp(scores - row_max)
    attn_prob = raised / jnp.sum(raised, axis=(2, 3), keepdims=True)
    rounded = lax.optimization_barrier(attn_prob.astype(jnp.bfloat16)).astype(jnp.float32)
    attended = jnp.einsum('hikj,kjhd->ihd', rounded, value_f)
    row_delta = jnp.sum(grad_f * attended, axis=2)
    prob_grad = jnp.einsum('ihd,kjhd->hikj', grad_f, value_f)
    score_grad = attn_prob * (prob_grad - jnp.transpose(row_delta)[:, :, None, None]) * scaling
    score_grad = lax.optimization_barrier(score_grad.astype(jnp.bfloat16)).astype(jnp.float32)
    query_part = jnp.einsum('hikj,kjhd->ihd', score_grad, key_f)
    key_part = jnp.einsum('hikj,ihd->kjhd', score_grad, query_f)
    value_part = jnp.einsum('hikj,ihd->kjhd', rounded, grad_f)
    return query_part, key_part, value_part


def reference(queries, keys, values, out_grad, block_lists):
    head_size = D // HEADS
    qblock_count = TOKENS // BLOCK
    per_view = NBLK * N_SUB
    query_blocks = queries.reshape(qblock_count, BLOCK, HEADS, head_size)
    key_blocks = keys.reshape(qblock_count, BLOCK, HEADS, head_size)
    value_blocks = values.reshape(qblock_count, BLOCK, HEADS, head_size)
    grad_blocks = out_grad.reshape(qblock_count, BLOCK, HEADS, head_size)
    token_iota = jnp.arange(BLOCK, dtype=jnp.int32)

    def one_block(running, block_index):
        key_acc, value_acc = running
        list_ids = block_lists[block_index]
        is_live = list_ids >= 0
        prev_ok = (block_index % per_view) != 0
        chosen = jnp.concatenate([
            jnp.reshape(jnp.maximum(block_index - 1, 0), (1,)).astype(jnp.int32),
            jnp.reshape(block_index, (1,)).astype(jnp.int32),
            jnp.where(is_live, list_ids, 0).astype(jnp.int32)])
        usable = jnp.concatenate([jnp.reshape(prev_ok, (1,)), jnp.ones((1,), bool), is_live])
        query_part, key_part, value_part = block_backward(
            query_blocks[block_index], grad_blocks[block_index],
            key_blocks[chosen], value_blocks[chosen], usable)
        row_ids = (chosen[:, None] * BLOCK + token_iota[None, :]).reshape(-1)
        key_acc = key_acc.at[row_ids].add(key_part.reshape(-1, D))
        value_acc = value_acc.at[row_ids].add(value_part.reshape(-1, D))
        return (key_acc, value_acc), query_part.astype(jnp.bfloat16)

    start = (jnp.zeros((TOKENS, D), jnp.float32), jnp.zeros((TOKENS, D), jnp.float32))
    (key_acc, value_acc), query_parts = lax.scan(one_block, start, jnp.arange(qblock_count, dtype=jnp.int32))
    query_grad = query_parts.reshape(TOKENS, D)
    return query_grad, key_acc.astype(jnp.bfloat16), value_acc.astype(jnp.bfloat16)
```

```python
import jax
import jax.numpy as jnp
from jax import lax
from jax.experimental import pallas as pl
from jax.experimental.pallas import tpu as pltpu
from jax.sharding import PartitionSpec as P

MESH = pl.DeviceIdType.MESH
F32 = jnp.float32
BF16 = jnp.bfloat16
SIDE = 4
BLK = 128
WIDTH = 512
HALF = 256
PAIRS = 4
LOCAL = 16
ENTRIES = 19
FAR = 1e30


def nt(a, b):
    return lax.dot_general(a, b, (((1,), (1,)), ((), ())), preferred_element_type=F32)


def nn(a, b):
    return lax.dot_general(a, b, (((1,), (0,)), ((), ())), preferred_element_type=F32)


def tn(a, b):
    return lax.dot_general(a, b, (((0,), (0,)), ((), ())), preferred_element_type=F32)


def pick(first, second, second_weight):
    return first * (1 - second_weight) + second * second_weight


def kernel(
    lists_ref,
    q_ref,
    k_ref,
    v_ref,
    g_ref,
    dq_ref,
    dk_ref,
    dv_ref,
    qs_ref,
    meta_ref,
    meta_x,
    meta_y,
    near,
    stage,
    kv_in,
    qg_in,
    raised_buf,
    grad_buf,
    max_buf,
    sum_buf,
    scale_buf,
    delta_buf,
    stat_out,
    stat_in,
    dq_acc,
    dk_acc,
    dv_acc,
    meta_ss,
    meta_rs,
    near_ss,
    near_rs,
    far_ss,
    far_rs,
    win_ss,
    win_rs,
    stat_ss,
    stat_rs,
):
    me = lax.axis_index("views")
    band = lax.axis_index("sub")
    bands = lax.axis_size("sub")
    x, y = me // SIDE, me % SIDE
    after = lax.rem(band + 1, bands)
    ahead = lax.rem(band + bands - 1, bands)

    def view(a, b):
        return lax.rem(x + (a % SIDE), SIDE) * SIDE + lax.rem(y + (b % SIDE), SIDE)

    offsets = [(a, b) for a in range(SIDE) for b in range(SIDE) if (a, b) != (0, 0)]

    barrier = pltpu.get_barrier_semaphore()
    for a, b in offsets:
        pl.semaphore_signal(
            barrier, inc=1, device_id={"views": view(a, b)}, device_id_type=MESH
        )
    for s in (after, ahead):
        pl.semaphore_signal(barrier, inc=1, device_id={"sub": s}, device_id_type=MESH)

    lists = lists_ref[...]
    views = lax.broadcasted_iota(jnp.int32, (16, 16), 0)
    found = []
    for row in range(2):
        ids = jnp.broadcast_to(lists[row : row + 1, :], (16, 16))
        hit = (ids >= 0) & ((ids >> 4) == views)
        live = jnp.sum(jnp.where(hit, 1.0, 0.0), axis=1, keepdims=True)
        odd = jnp.sum(jnp.where(hit & ((ids & 1) == 1), 1.0, 0.0), axis=1, keepdims=True)
        found.append((live, odd))
    meta_ref[0] = jnp.broadcast_to(found[0][1] + found[1][1], (16, 128))
    meta_ref[1] = jnp.broadcast_to(found[1][0], (16, 128))
    meta_ref[2] = jnp.broadcast_to(found[0][0] + found[1][0], (16, 128))
    qs_ref[...] = q_ref[...] * jnp.asarray(0.125, BF16)

    pl.semaphore_wait(barrier, 17)

    sent = []

    def copy(src, dst, ss, rs, **to):
        c = pltpu.make_async_remote_copy(
            src_ref=src,
            dst_ref=dst,
            send_sem=ss,
            recv_sem=rs,
            device_id=to,
            device_id_type=MESH,
        )
        c.start()
        sent.append(c)
        return c

    metas = {}
    for d in (1, 3, 2):
        metas["x", d] = copy(
            meta_ref.at[0:2],
            meta_x.at[d - 1],
            meta_ss.at[0, d - 1],
            meta_rs.at[0, d - 1],
            views=view(-d, 0),
        )
        metas["y", d] = copy(
            meta_ref.at[0:2],
            meta_y.at[d - 1],
            meta_ss.at[1, d - 1],
            meta_rs.at[1, d - 1],
            views=view(0, -d),
        )

    own = ((k_ref, v_ref), (qs_ref, g_ref))
    nears = {}

    def send_near(group):
        for d in (1, 3, 2):
            for arr in range(2):
                for half in range(2):
                    nears[group, half, d, arr] = copy(
                        own[group][arr].at[:, half * HALF : (half + 1) * HALF],
                        near.at[group, half, d - 1, arr],
                        near_ss.at[group, half, d - 1, arr],
                        near_rs.at[group, half, d - 1, arr],
                        views=view(d, 0) if half == 0 else view(0, d),
                    )

    wins = {}

    def send_window(group):
        rows = slice(BLK, 2 * BLK) if group == 0 else slice(0, BLK)
        target = kv_in if group == 0 else qg_in
        for arr in range(2):
            for half in range(2):
                wins[group, half, arr] = copy(
                    own[group][arr].at[rows, half * HALF : (half + 1) * HALF],
                    target.at[0, half, arr],
                    win_ss.at[group, half, arr],
                    win_rs.at[group, half, arr],
                    sub=after if group == 0 else ahead,
                )

    send_near(0)
    send_window(0)
    send_window(1)
    send_near(1)

    lane = lax.broadcasted_iota(jnp.int32, (1, 128), 1)
    low = jnp.where(lane < 64, 1.0, 0.0)
    low16, high16 = low.astype(BF16), (1.0 - low).astype(BF16)

    def stack(piece):
        return jnp.concatenate([piece * low16, piece * high16], axis=0)

    def wide(row):
        return jnp.concatenate([row, row], axis=1)

    def forward(entry, p, qp, gp, kp, vp):
        scores = nt(kp, stack(qp))
        grads = nt(vp, stack(gp))
        top = jnp.max(scores, axis=0, keepdims=True)
        raised = jnp.exp(scores - top)
        raised_buf[entry, p] = raised
        grad_buf[entry, p] = grads
        max_buf[entry, p : p + 1, :] = top
        sum_buf[entry, p : p + 1, :] = jnp.sum(raised, axis=0, keepdims=True)

    def local_forward(n, carry):
        q_rows = pl.ds(pl.multiple_of(jnp.minimum(n, 1) * BLK, BLK), BLK)
        k_rows = pl.ds(pl.multiple_of((n // 2) * BLK, BLK), BLK)
        for p in range(PAIRS):
            cols = slice(p * 128, (p + 1) * 128)
            forward(
                LOCAL + n,
                p,
                qs_ref[q_rows, cols],
                g_ref[q_rows, cols],
                k_ref[k_rows, cols],
                v_ref[k_rows, cols],
            )
        return carry

    lax.fori_loop(0, 3, local_forward, 0)

    for c in metas.values():
        c.wait_recv()

    def meta_of(axis, d, plane, row):
        if d % SIDE == 0:
            got = meta_ref[plane, pl.ds(row, 1), :]
        elif axis == "x":
            got = meta_x[d % SIDE - 1, plane, pl.ds(row, 1), :]
        else:
            got = meta_y[d % SIDE - 1, plane, pl.ds(row, 1), :]
        return got.astype(BF16)

    def want(group, half, j, d):
        if group == 0 and half == 0:
            return meta_of("y", d, 0, view(-j, 0))
        if group == 0:
            return meta_of("x", d, 0, view(0, -j))
        if half == 0:
            return meta_of("x", -j, 1, view(0, d))
        return meta_of("y", -j, 1, view(d, 0))

    fars = {}

    def send_far(group, j):
        for half in range(2):
            if j:
                for arr in range(2):
                    nears[group, half, j, arr].wait_recv()
            target = kv_in if group == 0 else qg_in
            for d in (1, 3, 2, 0):
                if d == 0 and j == 0:
                    continue
                slot = j * SIDE + d if half == 0 else d * SIDE + j
                weight = want(group, half, j, d)
                weight = wide(weight)
                for arr in range(2):
                    if j:
                        first = near[group, half, j - 1, arr, 0:BLK, :]
                        second = near[group, half, j - 1, arr, BLK : 2 * BLK, :]
                    else:
                        cols = slice(half * HALF, (half + 1) * HALF)
                        first = own[group][arr][0:BLK, cols]
                        second = own[group][arr][BLK : 2 * BLK, cols]
                    chosen = pick(first, second, weight)
                    if d:
                        stage[group, half, j, d - 1, arr] = chosen
                    else:
                        target[slot, half, arr] = chosen
                if d:
                    fars[group, half, slot] = copy(
                        stage.at[group, half, j, d - 1],
                        target.at[slot, half],
                        far_ss.at[group, half, j, d - 1],
                        far_rs.at[group, half, j, d - 1],
                        views=view(0, d) if half == 0 else view(d, 0),
                    )

    for j in (0, 1, 3, 2):
        send_far(0, j)
    for j in (0, 1, 3, 2):
        send_far(1, j)

    def view_of_slot(i):
        return lax.rem(x + SIDE - i // SIDE, SIDE) * SIDE + lax.rem(y + SIDE - i % SIDE, SIDE)

    def remote_forward(i, carry):
        weight = meta_ref[1, pl.ds(view_of_slot(i), 1), :].astype(BF16)
        for p in range(PAIRS):
            cols = slice(p * 128, (p + 1) * 128)
            inner = slice((p % 2) * 128, (p % 2 + 1) * 128)
            forward(
                i,
                p,
                pick(qs_ref[0:BLK, cols], qs_ref[BLK : 2 * BLK, cols], weight),
                pick(g_ref[0:BLK, cols], g_ref[BLK : 2 * BLK, cols], weight),
                kv_in[i, p // 2, 0, :, inner],
                kv_in[i, p // 2, 1, :, inner],
            )
        return carry

    for c in (wins[0, h, r] for h in range(2) for r in range(2)):
        c.wait_recv()
    for a in (0, 1, 3, 2):
        for b in range(SIDE):
            slot = a * SIDE + b
            for half in range(2):
                if (0, half, slot) in fars:
                    fars[0, half, slot].wait_recv()
        lax.fori_loop(a * SIDE, (a + 1) * SIDE, remote_forward, 0)

    has_prev = jnp.where(band > 0, 1.0, 0.0)
    ones = jnp.full((1, HALF), 1.0, F32)
    uses = []
    for e in range(ENTRIES):
        if e == 0:
            uses.append((ones * has_prev, ones * 0.0))
        elif e < LOCAL:
            row = view(-(e // SIDE), -(e % SIDE))
            second = wide(meta_ref[1, pl.ds(row, 1), :])
            live = wide(meta_ref[2, pl.ds(row, 1), :])
            uses.append((live * (1.0 - second), live * second))
        else:
            second = ones * (0.0 if e == LOCAL else 1.0)
            uses.append((1.0 - second, second))
    tops, invs = [], []
    for blk in range(2):
        top = jnp.full((PAIRS, HALF), -FAR, F32)
        for e in range(ENTRIES):
            top = jnp.maximum(top, max_buf[e] + (uses[e][blk] - 1.0) * FAR)
        tops.append(top)
        total = jnp.zeros((PAIRS, HALF), F32)
        for e in range(ENTRIES):
            total += uses[e][blk] * sum_buf[e] * jnp.exp(jnp.minimum(max_buf[e] - top, 0.0))
        invs.append(1.0 / total)
    for e in range(ENTRIES):
        scale_buf[e] = sum(
            uses[e][blk] * jnp.exp(jnp.minimum(max_buf[e] - tops[blk], 0.0)) * invs[blk]
            for blk in range(2)
        )

    def delta_part(e, carry):
        for p in range(PAIRS):
            prob = raised_buf[e, p] * scale_buf[e, p : p + 1, :]
            rounded = prob.astype(BF16).astype(F32)
            delta_buf[e, p : p + 1, :] = jnp.sum(rounded * grad_buf[e, p], axis=0, keepdims=True)
        return carry

    lax.fori_loop(0, ENTRIES, delta_part, 0)
    deltas = [
        sum(uses[e][blk] * delta_buf[e] for e in range(ENTRIES)) for blk in range(2)
    ]
    stats = {}
    for e in range(ENTRIES):
        first, second = uses[e]
        delta = first * deltas[0] + second * deltas[1]
        delta_buf[e] = delta
        if e < LOCAL:
            a, b = e // SIDE, e % SIDE
            stat_out[e, 0:4, :] = (
                first * tops[0] + second * tops[1] + (1.0 - first - second) * FAR
            )
            stat_out[e, 4:8, :] = first * invs[0] + second * invs[1]
            stat_out[e, 8:12, :] = delta
            if e:
                stat_out[e, 12:16, :] = jnp.broadcast_to(
                    wide(meta_ref[0, pl.ds(view(-a, -b), 1), :]), (4, HALF)
                )
            else:
                stat_out[e, 12:16, :] = jnp.ones((4, HALF), F32)
            slot = (-a % SIDE) * SIDE + (-b % SIDE)
            to = {"views": view(-a, -b)} if e else {"sub": ahead}
            stats[slot] = copy(
                stat_out.at[e], stat_in.at[slot], stat_ss.at[slot], stat_rs.at[slot], **to
            )

    dq_acc[...] = jnp.zeros_like(dq_acc)
    dk_acc[...] = jnp.zeros_like(dk_acc)
    dv_acc[...] = jnp.zeros_like(dv_acc)

    def score_gradient(e, p):
        prob = raised_buf[e, p] * scale_buf[e, p : p + 1, :]
        return prob, (prob * (grad_buf[e, p] - delta_buf[e, p : p + 1, :])).astype(BF16)

    def halves(both):
        return jnp.where(lane < 64, both[0:BLK, :], both[BLK : 2 * BLK, :])

    def local_backward(n, carry):
        q_rows = pl.ds(pl.multiple_of(jnp.minimum(n, 1) * BLK, BLK), BLK)
        k_rows = pl.ds(pl.multiple_of((n // 2) * BLK, BLK), BLK)
        for p in range(PAIRS):
            cols = slice(p * 128, (p + 1) * 128)
            prob, ds = score_gradient(LOCAL + n, p)
            dq_acc[q_rows, cols] += halves(tn(ds, k_ref[k_rows, cols]))
            dk_acc[k_rows, cols] += nn(ds, stack(qs_ref[q_rows, cols]))
            dv_acc[k_rows, cols] += nn(prob.astype(BF16), stack(g_ref[q_rows, cols]))
        return carry

    lax.fori_loop(0, 3, local_backward, 0)

    def remote_backward(i, carry):
        weight = meta_ref[1, pl.ds(view_of_slot(i), 1), :]
        weight = jnp.where(i == 0, 0.0, weight)
        for p in range(PAIRS):
            cols = slice(p * 128, (p + 1) * 128)
            inner = slice((p % 2) * 128, (p % 2 + 1) * 128)
            _, ds = score_gradient(i, p)
            part = halves(tn(ds, kv_in[i, p // 2, 0, :, inner]))
            dq_acc[0:BLK, cols] += part * (1.0 - weight)
            dq_acc[BLK : 2 * BLK, cols] += part * weight
        return carry

    lax.fori_loop(0, LOCAL, remote_backward, 0)
    dq_ref[...] = (dq_acc[...] * 0.125).astype(BF16)

    def owner_backward(i, carry):
        weight = stat_in[i, 12:13, 0:128]
        weight16 = weight.astype(BF16)
        for p in range(PAIRS):
            cols = slice(p * 128, (p + 1) * 128)
            inner = slice((p % 2) * 128, (p % 2 + 1) * 128)
            kp = pick(k_ref[0:BLK, cols], k_ref[BLK : 2 * BLK, cols], weight16)
            vp = pick(v_ref[0:BLK, cols], v_ref[BLK : 2 * BLK, cols], weight16)
            qp = stack(qg_in[i, p // 2, 0, :, inner])
            gp = stack(qg_in[i, p // 2, 1, :, inner])
            prob = jnp.exp(nt(kp, qp) - stat_in[i, p : p + 1, :]) * stat_in[i, 4 + p : 5 + p, :]
            ds = (prob * (nt(vp, gp) - stat_in[i, 8 + p : 9 + p, :])).astype(BF16)
            dk = nn(ds, qp)
            dv = nn(prob.astype(BF16), gp)
            dk_acc[0:BLK, cols] += dk * (1.0 - weight)
            dk_acc[BLK : 2 * BLK, cols] += dk * weight
            dv_acc[0:BLK, cols] += dv * (1.0 - weight)
            dv_acc[BLK : 2 * BLK, cols] += dv * weight
        return carry

    for c in (wins[1, h, r] for h in range(2) for r in range(2)):
        c.wait_recv()
    for a in (0, 1, 3, 2):
        for b in range(SIDE):
            slot = a * SIDE + b
            stats[slot].wait_recv()
            for half in range(2):
                if (1, half, slot) in fars:
                    fars[1, half, slot].wait_recv()
        lax.fori_loop(a * SIDE, (a + 1) * SIDE, owner_backward, 0)

    dk_ref[...] = dk_acc[...].astype(BF16)
    dv_ref[...] = dv_acc[...].astype(BF16)
    for c in sent:
        c.wait_send()


def shards(queries, keys, values, out_grad, block_lists):
    vmem = pl.BlockSpec(memory_space=pltpu.VMEM)
    rows = 2 * BLK
    dma = pltpu.SemaphoreType.DMA
    stat_rows = (ENTRIES, PAIRS, HALF)
    return pl.pallas_call(
        kernel,
        out_shape=[jax.ShapeDtypeStruct((rows, WIDTH), BF16)] * 3,
        in_specs=[vmem] * 5,
        out_specs=[vmem] * 3,
        scratch_shapes=[
            pltpu.VMEM((rows, WIDTH), BF16),
            pltpu.VMEM((3, 16, 128), F32),
            pltpu.VMEM((3, 2, 16, 128), F32),
            pltpu.VMEM((3, 2, 16, 128), F32),
            pltpu.VMEM((2, 2, 3, 2, rows, HALF), BF16),
            pltpu.VMEM((2, 2, 4, 3, 2, BLK, HALF), BF16),
            pltpu.VMEM((16, 2, 2, BLK, HALF), BF16),
            pltpu.VMEM((16, 2, 2, BLK, HALF), BF16),
            pltpu.VMEM((ENTRIES, PAIRS, BLK, HALF), F32),
            pltpu.VMEM((ENTRIES, PAIRS, BLK, HALF), F32),
            pltpu.VMEM(stat_rows, F32),
            pltpu.VMEM(stat_rows, F32),
            pltpu.VMEM(stat_rows, F32),
            pltpu.VMEM(stat_rows, F32),
            pltpu.VMEM((16, 16, HALF), F32),
            pltpu.VMEM((16, 16, HALF), F32),
            pltpu.VMEM((rows, WIDTH), F32),
            pltpu.VMEM((rows, WIDTH), F32),
            pltpu.VMEM((rows, WIDTH), F32),
            dma((2, 3)),
            dma((2, 3)),
            dma((2, 2, 3, 2)),
            dma((2, 2, 3, 2)),
            dma((2, 2, 4, 3)),
            dma((2, 2, 4, 3)),
            dma((2, 2, 2)),
            dma((2, 2, 2)),
            dma((16,)),
            dma((16,)),
        ],
        compiler_params=pltpu.CompilerParams(
            collective_id=0, has_side_effects=True, vmem_limit_bytes=60 * 1024 * 1024
        ),
    )(block_lists, queries, keys, values, out_grad)


def solution(mesh):
    spec = P(("views", "sub"), None)
    return jax.shard_map(
        shards,
        mesh=mesh,
        in_specs=(spec,) * 5,
        out_specs=(spec,) * 3,
        check_vma=False,
    )
```

```python
import functools

import jax
import jax.numpy as jnp
from jax import lax
from jax.experimental import pallas as pl
from jax.experimental.pallas import tpu as pltpu
from jax.sharding import PartitionSpec as P

MESH = pl.DeviceIdType.MESH
F32 = jnp.float32
BF16 = jnp.bfloat16
SIDE = 4
BLK = 128
WIDTH = 512
HALF = 256
PAIRS = 4
LOCAL = 16
ENTRIES = 19
FAR = 1e30


def nt(a, b):
    return lax.dot_general(a, b, (((1,), (1,)), ((), ())), preferred_element_type=F32)


def nn(a, b):
    return lax.dot_general(a, b, (((1,), (0,)), ((), ())), preferred_element_type=F32)


def tn(a, b):
    return lax.dot_general(a, b, (((0,), (0,)), ((), ())), preferred_element_type=F32)


def pick(first, second, second_weight):
    return first * (1 - second_weight) + second * second_weight


def kernel(
    lists_ref,
    q_ref,
    k_ref,
    v_ref,
    g_ref,
    dq_ref,
    dk_ref,
    dv_ref,
    qs_ref,
    meta_ref,
    meta_x,
    meta_y,
    near,
    stage,
    kv_in,
    qg_in,
    raised_buf,
    grad_buf,
    max_buf,
    sum_buf,
    scale_buf,
    delta_buf,
    stat_out,
    stat_in,
    dq_acc,
    dk_acc,
    dv_acc,
    meta_ss,
    meta_rs,
    near_ss,
    near_rs,
    far_ss,
    far_rs,
    win_ss,
    win_rs,
    stat_ss,
    stat_rs,
):
    me = lax.axis_index("views")
    band = lax.axis_index("sub")
    bands = lax.axis_size("sub")
    x, y = me // SIDE, me % SIDE
    after = lax.rem(band + 1, bands)
    ahead = lax.rem(band + bands - 1, bands)

    def view(a, b):
        return lax.rem(x + (a % SIDE), SIDE) * SIDE + lax.rem(y + (b % SIDE), SIDE)

    offsets = [(a, b) for a in range(SIDE) for b in range(SIDE) if (a, b) != (0, 0)]

    barrier = pltpu.get_barrier_semaphore()
    for a, b in offsets:
        pl.semaphore_signal(
            barrier, inc=1, device_id={"views": view(a, b)}, device_id_type=MESH
        )
    for s in (after, ahead):
        pl.semaphore_signal(barrier, inc=1, device_id={"sub": s}, device_id_type=MESH)

    lists = lists_ref[...]
    views = lax.broadcasted_iota(jnp.int32, (16, 16), 0)
    found = []
    for row in range(2):
        ids = jnp.broadcast_to(lists[row : row + 1, :], (16, 16))
        hit = (ids >= 0) & ((ids >> 4) == views)
        live = jnp.sum(jnp.where(hit, 1.0, 0.0), axis=1, keepdims=True)
        odd = jnp.sum(jnp.where(hit & ((ids & 1) == 1), 1.0, 0.0), axis=1, keepdims=True)
        found.append((live, odd))
    meta_ref[0] = jnp.broadcast_to(found[0][1] + found[1][1], (16, 128))
    meta_ref[1] = jnp.broadcast_to(found[1][0], (16, 128))
    meta_ref[2] = jnp.broadcast_to(found[0][0] + found[1][0], (16, 128))
    qs_ref[...] = q_ref[...] * jnp.asarray(0.125, BF16)

    pl.semaphore_wait(barrier, 17)

    sent = []

    def copy(src, dst, ss, rs, **to):
        c = pltpu.make_async_remote_copy(
            src_ref=src,
            dst_ref=dst,
            send_sem=ss,
            recv_sem=rs,
            device_id=to,
            device_id_type=MESH,
        )
        c.start()
        sent.append(c)
        return c

    metas = {}
    for d in (1, 3, 2):
        metas["x", d] = copy(
            meta_ref.at[0:2],
            meta_x.at[d - 1],
            meta_ss.at[0, d - 1],
            meta_rs.at[0, d - 1],
            views=view(-d, 0),
        )
        metas["y", d] = copy(
            meta_ref.at[0:2],
            meta_y.at[d - 1],
            meta_ss.at[1, d - 1],
            meta_rs.at[1, d - 1],
            views=view(0, -d),
        )

    own = ((k_ref, v_ref), (qs_ref, g_ref))
    nears = {}

    def send_near(group):
        for arr in range(2):
            for d in (1, 3):
                for half in range(2):
                    nears[group, half, d, arr] = copy(
                        own[group][arr].at[:, half * HALF : (half + 1) * HALF],
                        near.at[group, half, d - 1, arr],
                        near_ss.at[group, half, d - 1, arr],
                        near_rs.at[group, half, d - 1, arr],
                        views=view(d, 0) if half == 0 else view(0, d),
                    )

    passed = {}

    def pass_on(group):
        for arr in range(2):
            for d in (1, 3):
                for half in range(2):
                    nears[group, half, d, arr].wait_recv()
                    rows = slice(0, BLK) if d == 1 else slice(BLK, 2 * BLK)
                    passed[group, half, d, arr] = copy(
                        near.at[group, half, d - 1, arr, rows, :],
                        near.at[group, half, 1, arr, rows, :],
                        near_ss.at[group, half, d, arr],
                        near_rs.at[group, half, d, arr],
                        views=view(d, 0) if half == 0 else view(0, d),
                    )

    wins = {}

    def send_window(group):
        rows = slice(BLK, 2 * BLK) if group == 0 else slice(0, BLK)
        target = kv_in if group == 0 else qg_in
        for arr in range(2):
            for half in range(2):
                wins[group, half, arr] = copy(
                    own[group][arr].at[rows, half * HALF : (half + 1) * HALF],
                    target.at[0, half, arr],
                    win_ss.at[group, half, arr],
                    win_rs.at[group, half, arr],
                    sub=after if group == 0 else ahead,
                )

    send_near(0)
    send_window(0)
    send_window(1)

    lane = lax.broadcasted_iota(jnp.int32, (1, 128), 1)
    low = jnp.where(lane < 64, 1.0, 0.0)
    low16, high16 = low.astype(BF16), (1.0 - low).astype(BF16)

    def stack(piece):
        return jnp.concatenate([piece * low16, piece * high16], axis=0)

    def wide(row):
        return jnp.concatenate([row, row], axis=1)

    def forward(entry, p, qp, gp, kp, vp):
        scores = nt(kp, stack(qp))
        grads = nt(vp, stack(gp))
        top = jnp.max(scores, axis=0, keepdims=True)
        raised = jnp.exp(scores - top)
        raised_buf[entry, p] = raised
        grad_buf[entry, p] = grads
        max_buf[entry, p : p + 1, :] = top
        sum_buf[entry, p : p + 1, :] = jnp.sum(raised, axis=0, keepdims=True)

    def local_forward(n, carry):
        q_rows = pl.ds(pl.multiple_of(jnp.minimum(n, 1) * BLK, BLK), BLK)
        k_rows = pl.ds(pl.multiple_of((n // 2) * BLK, BLK), BLK)
        for p in range(PAIRS):
            cols = slice(p * 128, (p + 1) * 128)
            forward(
                LOCAL + n,
                p,
                qs_ref[q_rows, cols],
                g_ref[q_rows, cols],
                k_ref[k_rows, cols],
                v_ref[k_rows, cols],
            )
        return carry

    lax.fori_loop(0, 3, local_forward, 0)

    for c in metas.values():
        c.wait_recv()

    def meta_of(axis, d, plane, row):
        if d % SIDE == 0:
            got = meta_ref[plane, pl.ds(row, 1), :]
        elif axis == "x":
            got = meta_x[d % SIDE - 1, plane, pl.ds(row, 1), :]
        else:
            got = meta_y[d % SIDE - 1, plane, pl.ds(row, 1), :]
        return got.astype(BF16)

    def want(group, half, j, d):
        if group == 0 and half == 0:
            return meta_of("y", d, 0, view(-j, 0))
        if group == 0:
            return meta_of("x", d, 0, view(0, -j))
        if half == 0:
            return meta_of("x", -j, 1, view(0, d))
        return meta_of("y", -j, 1, view(d, 0))

    fars = {}

    def send_far(group, j):
        if j == 2:
            for c in (passed[group, h, d, r] for h in range(2) for d in (1, 3) for r in range(2)):
                c.wait_recv()
        target = kv_in if group == 0 else qg_in
        for d in (1, 3, 2, 0):
            for half in range(2):
                if d == 0 and j == 0:
                    continue
                slot = j * SIDE + d if half == 0 else d * SIDE + j
                weight = wide(want(group, half, j, d))
                for arr in range(2):
                    if j:
                        first = near[group, half, j - 1, arr, 0:BLK, :]
                        second = near[group, half, j - 1, arr, BLK : 2 * BLK, :]
                    else:
                        cols = slice(half * HALF, (half + 1) * HALF)
                        first = own[group][arr][0:BLK, cols]
                        second = own[group][arr][BLK : 2 * BLK, cols]
                    chosen = pick(first, second, weight)
                    if d:
                        stage[group, half, j, d - 1, arr] = chosen
                    else:
                        target[slot, half, arr] = chosen
                if d:
                    fars[group, half, slot] = copy(
                        stage.at[group, half, j, d - 1],
                        target.at[slot, half],
                        far_ss.at[group, half, j, d - 1],
                        far_rs.at[group, half, j, d - 1],
                        views=view(0, d) if half == 0 else view(d, 0),
                    )

    send_far(0, 0)
    pass_on(0)
    send_far(0, 1)
    send_far(0, 3)
    send_far(0, 2)
    send_near(1)

    def view_of_slot(i):
        return lax.rem(x + SIDE - i // SIDE, SIDE) * SIDE + lax.rem(y + SIDE - i % SIDE, SIDE)

    def slot_of(half, j, n):
        return j * SIDE + n if half == 0 else n * SIDE + j

    def remote_forward(half, j, n, carry):
        i = slot_of(half, j, n)
        weight = meta_ref[1, pl.ds(view_of_slot(i), 1), :].astype(BF16)
        weight = weight * jnp.where(i == 0, 0.0, 1.0).astype(BF16)
        for p in (2 * half, 2 * half + 1):
            cols = slice(p * 128, (p + 1) * 128)
            inner = slice((p % 2) * 128, (p % 2 + 1) * 128)
            forward(
                i,
                p,
                pick(qs_ref[0:BLK, cols], qs_ref[BLK : 2 * BLK, cols], weight),
                pick(g_ref[0:BLK, cols], g_ref[BLK : 2 * BLK, cols], weight),
                kv_in[i, half, 0, :, inner],
                kv_in[i, half, 1, :, inner],
            )
        return carry

    def wait_items(group, half, j):
        if j == 0:
            for arr in range(2):
                wins[group, half, arr].wait_recv()
        for n in range(1, SIDE):
            fars[group, half, slot_of(half, j, n)].wait_recv()

    for j in (0, 1, 3, 2):
        for half in range(2):
            wait_items(0, half, j)
            lax.fori_loop(0, SIDE, functools.partial(remote_forward, half, j), 0, unroll=4)
        if j == 1:
            send_far(1, 0)

    has_prev = jnp.where(band > 0, 1.0, 0.0)
    ones = jnp.full((1, HALF), 1.0, F32)
    uses = []
    for e in range(ENTRIES):
        if e == 0:
            uses.append((ones * has_prev, ones * 0.0))
        elif e < LOCAL:
            row = view(-(e // SIDE), -(e % SIDE))
            second = wide(meta_ref[1, pl.ds(row, 1), :])
            live = wide(meta_ref[2, pl.ds(row, 1), :])
            uses.append((live * (1.0 - second), live * second))
        else:
            second = ones * (0.0 if e == LOCAL else 1.0)
            uses.append((1.0 - second, second))
    tops, invs = [], []
    for blk in range(2):
        top = jnp.full((PAIRS, HALF), -FAR, F32)
        for e in range(ENTRIES):
            top = jnp.maximum(top, max_buf[e] + (uses[e][blk] - 1.0) * FAR)
        tops.append(top)
        total = jnp.zeros((PAIRS, HALF), F32)
        for e in range(ENTRIES):
            total += uses[e][blk] * sum_buf[e] * jnp.exp(jnp.minimum(max_buf[e] - top, 0.0))
        invs.append(1.0 / total)
    for e in range(ENTRIES):
        scale_buf[e] = sum(
            uses[e][blk] * jnp.exp(jnp.minimum(max_buf[e] - tops[blk], 0.0)) * invs[blk]
            for blk in range(2)
        )

    def delta_part(e, carry):
        for p in range(PAIRS):
            prob = raised_buf[e, p] * scale_buf[e, p : p + 1, :]
            rounded = prob.astype(BF16).astype(F32)
            delta_buf[e, p : p + 1, :] = jnp.sum(rounded * grad_buf[e, p], axis=0, keepdims=True)
        return carry

    lax.fori_loop(0, ENTRIES, delta_part, 0)
    deltas = [
        sum(uses[e][blk] * delta_buf[e] for e in range(ENTRIES)) for blk in range(2)
    ]
    stats = {}
    for e in range(ENTRIES):
        first, second = uses[e]
        delta = first * deltas[0] + second * deltas[1]
        delta_buf[e] = delta
        if e < LOCAL:
            a, b = e // SIDE, e % SIDE
            stat_out[e, 0:4, :] = (
                first * tops[0] + second * tops[1] + (1.0 - first - second) * FAR
            )
            stat_out[e, 4:8, :] = first * invs[0] + second * invs[1]
            stat_out[e, 8:12, :] = delta
            if e:
                stat_out[e, 12:16, :] = jnp.broadcast_to(
                    wide(meta_ref[0, pl.ds(view(-a, -b), 1), :]), (4, HALF)
                )
            else:
                stat_out[e, 12:16, :] = jnp.ones((4, HALF), F32)
            slot = (-a % SIDE) * SIDE + (-b % SIDE)
            to = {"views": view(-a, -b)} if e else {"sub": ahead}
            stats[slot] = copy(
                stat_out.at[e], stat_in.at[slot], stat_ss.at[slot], stat_rs.at[slot], **to
            )

    pass_on(1)
    send_far(1, 1)
    send_far(1, 3)

    dq_acc[...] = jnp.zeros_like(dq_acc)
    dk_acc[...] = jnp.zeros_like(dk_acc)
    dv_acc[...] = jnp.zeros_like(dv_acc)

    def score_gradient(e, p):
        prob = raised_buf[e, p] * scale_buf[e, p : p + 1, :]
        return prob, (prob * (grad_buf[e, p] - delta_buf[e, p : p + 1, :])).astype(BF16)

    def halves(both):
        return jnp.where(lane < 64, both[0:BLK, :], both[BLK : 2 * BLK, :])

    def local_backward(n, carry):
        q_rows = pl.ds(pl.multiple_of(jnp.minimum(n, 1) * BLK, BLK), BLK)
        k_rows = pl.ds(pl.multiple_of((n // 2) * BLK, BLK), BLK)
        for p in range(PAIRS):
            cols = slice(p * 128, (p + 1) * 128)
            prob, ds = score_gradient(LOCAL + n, p)
            dq_acc[q_rows, cols] += halves(tn(ds, k_ref[k_rows, cols]))
            dk_acc[k_rows, cols] += nn(ds, stack(qs_ref[q_rows, cols]))
            dv_acc[k_rows, cols] += nn(prob.astype(BF16), stack(g_ref[q_rows, cols]))
        return carry

    lax.fori_loop(0, 3, local_backward, 0)

    def remote_backward(i, carry):
        weight = meta_ref[1, pl.ds(view_of_slot(i), 1), :]
        weight = jnp.where(i == 0, 0.0, weight)
        for p in range(PAIRS):
            cols = slice(p * 128, (p + 1) * 128)
            inner = slice((p % 2) * 128, (p % 2 + 1) * 128)
            _, ds = score_gradient(i, p)
            part = halves(tn(ds, kv_in[i, p // 2, 0, :, inner]))
            dq_acc[0:BLK, cols] += part * (1.0 - weight)
            dq_acc[BLK : 2 * BLK, cols] += part * weight
        return carry

    send_far(1, 2)
    lax.fori_loop(0, LOCAL, remote_backward, 0, unroll=2)
    dq_ref[...] = (dq_acc[...] * 0.125).astype(BF16)

    def owner_backward(half, j, n, carry):
        i = slot_of(half, j, n)
        weight = stat_in[i, 12:13, 0:128]
        weight16 = weight.astype(BF16)
        for p in (2 * half, 2 * half + 1):
            cols = slice(p * 128, (p + 1) * 128)
            inner = slice((p % 2) * 128, (p % 2 + 1) * 128)
            kp = pick(k_ref[0:BLK, cols], k_ref[BLK : 2 * BLK, cols], weight16)
            vp = pick(v_ref[0:BLK, cols], v_ref[BLK : 2 * BLK, cols], weight16)
            qp = stack(qg_in[i, half, 0, :, inner])
            gp = stack(qg_in[i, half, 1, :, inner])
            prob = jnp.exp(nt(kp, qp) - stat_in[i, p : p + 1, :]) * stat_in[i, 4 + p : 5 + p, :]
            ds = (prob * (nt(vp, gp) - stat_in[i, 8 + p : 9 + p, :])).astype(BF16)
            dk = nn(ds, qp)
            dv = nn(prob.astype(BF16), gp)
            dk_acc[0:BLK, cols] += dk * (1.0 - weight)
            dk_acc[BLK : 2 * BLK, cols] += dk * weight
            dv_acc[0:BLK, cols] += dv * (1.0 - weight)
            dv_acc[BLK : 2 * BLK, cols] += dv * weight
        return carry

    for c in stats.values():
        c.wait_recv()
    for j in (0, 1, 3, 2):
        for half in range(2):
            wait_items(1, half, j)
            lax.fori_loop(0, SIDE, functools.partial(owner_backward, half, j), 0, unroll=4)

    dk_ref[...] = dk_acc[...].astype(BF16)
    dv_ref[...] = dv_acc[...].astype(BF16)
    for c in sent:
        c.wait_send()


def shards(queries, keys, values, out_grad, block_lists):
    vmem = pl.BlockSpec(memory_space=pltpu.VMEM)
    rows = 2 * BLK
    dma = pltpu.SemaphoreType.DMA
    stat_rows = (ENTRIES, PAIRS, HALF)
    return pl.pallas_call(
        kernel,
        out_shape=[jax.ShapeDtypeStruct((rows, WIDTH), BF16)] * 3,
        in_specs=[vmem] * 5,
        out_specs=[vmem] * 3,
        scratch_shapes=[
            pltpu.VMEM((rows, WIDTH), BF16),
            pltpu.VMEM((3, 16, 128), F32),
            pltpu.VMEM((3, 2, 16, 128), F32),
            pltpu.VMEM((3, 2, 16, 128), F32),
            pltpu.VMEM((2, 2, 3, 2, rows, HALF), BF16),
            pltpu.VMEM((2, 2, 4, 3, 2, BLK, HALF), BF16),
            pltpu.VMEM((16, 2, 2, BLK, HALF), BF16),
            pltpu.VMEM((16, 2, 2, BLK, HALF), BF16),
            pltpu.VMEM((ENTRIES, PAIRS, BLK, HALF), F32),
            pltpu.VMEM((ENTRIES, PAIRS, BLK, HALF), F32),
            pltpu.VMEM(stat_rows, F32),
            pltpu.VMEM(stat_rows, F32),
            pltpu.VMEM(stat_rows, F32),
            pltpu.VMEM(stat_rows, F32),
            pltpu.VMEM((16, 16, HALF), F32),
            pltpu.VMEM((16, 16, HALF), F32),
            pltpu.VMEM((rows, WIDTH), F32),
            pltpu.VMEM((rows, WIDTH), F32),
            pltpu.VMEM((rows, WIDTH), F32),
            dma((2, 3)),
            dma((2, 3)),
            dma((2, 2, 4, 2)),
            dma((2, 2, 4, 2)),
            dma((2, 2, 4, 3)),
            dma((2, 2, 4, 3)),
            dma((2, 2, 2)),
            dma((2, 2, 2)),
            dma((16,)),
            dma((16,)),
        ],
        compiler_params=pltpu.CompilerParams(
            collective_id=0, has_side_effects=True, vmem_limit_bytes=60 * 1024 * 1024
        ),
    )(block_lists, queries, keys, values, out_grad)


def solution(mesh):
    spec = P(("views", "sub"), None)
    return jax.shard_map(
        shards,
        mesh=mesh,
        in_specs=(spec,) * 5,
        out_specs=(spec,) * 3,
        check_vma=False,
    )
```

```python
import jax
import jax.numpy as jnp
from jax import lax
from jax.experimental import pallas as pl
from jax.experimental.pallas import tpu as pltpu
from jax.sharding import PartitionSpec as P

MESH = pl.DeviceIdType.MESH
F32 = jnp.float32
BF16 = jnp.bfloat16
SIDE = 4
BLK = 128
WIDTH = 512
HALF = 256
PAIRS = 4
LOCAL = 16
ENTRIES = 19
FAR = 1e30


def nt(a, b):
    return lax.dot_general(a, b, (((1,), (1,)), ((), ())), preferred_element_type=F32)


def nn(a, b):
    return lax.dot_general(a, b, (((1,), (0,)), ((), ())), preferred_element_type=F32)


def tn(a, b):
    return lax.dot_general(a, b, (((0,), (0,)), ((), ())), preferred_element_type=F32)


def pick(first, second, second_weight):
    return first * (1 - second_weight) + second * second_weight


def kernel(
    lists_ref,
    q_hbm,
    k_hbm,
    v_hbm,
    g_hbm,
    dq_ref,
    dk_ref,
    dv_ref,
    q_ref,
    k_ref,
    v_ref,
    g_ref,
    qs_ref,
    meta_ref,
    meta_x,
    meta_y,
    near,
    stage,
    kv_in,
    qg_in,
    raised_buf,
    grad_buf,
    max_buf,
    sum_buf,
    scale_buf,
    delta_buf,
    stat_out,
    stat_in,
    dq_acc,
    dk_acc,
    dv_acc,
    meta_ss,
    meta_rs,
    near_ss,
    near_rs,
    far_ss,
    far_rs,
    win_ss,
    win_rs,
    stat_ss,
    stat_rs,
    load_sem,
):
    loads = []
    for n, (src, dst) in enumerate(
        ((k_hbm, k_ref), (v_hbm, v_ref), (q_hbm, q_ref), (g_hbm, g_ref))
    ):
        loads.append(pltpu.make_async_copy(src, dst, load_sem.at[n]))
        loads[n].start()
    me = lax.axis_index("views")
    band = lax.axis_index("sub")
    bands = lax.axis_size("sub")
    x, y = me // SIDE, me % SIDE
    after = lax.rem(band + 1, bands)
    ahead = lax.rem(band + bands - 1, bands)

    def view(a, b):
        return lax.rem(x + (a % SIDE), SIDE) * SIDE + lax.rem(y + (b % SIDE), SIDE)

    offsets = [(a, b) for a in range(SIDE) for b in range(SIDE) if (a, b) != (0, 0)]

    barrier = pltpu.get_barrier_semaphore()
    for a, b in offsets:
        pl.semaphore_signal(
            barrier, inc=1, device_id={"views": view(a, b)}, device_id_type=MESH
        )
    for s in (after, ahead):
        pl.semaphore_signal(barrier, inc=1, device_id={"sub": s}, device_id_type=MESH)

    lists = lists_ref[...]
    views = lax.broadcasted_iota(jnp.int32, (16, 16), 0)
    found = []
    for row in range(2):
        ids = jnp.broadcast_to(lists[row : row + 1, :], (16, 16))
        hit = (ids >= 0) & ((ids >> 4) == views)
        live = jnp.sum(jnp.where(hit, 1.0, 0.0), axis=1, keepdims=True)
        odd = jnp.sum(jnp.where(hit & ((ids & 1) == 1), 1.0, 0.0), axis=1, keepdims=True)
        found.append((live, odd))
    meta_ref[0] = jnp.broadcast_to(found[0][1] + found[1][1], (16, 128))
    meta_ref[1] = jnp.broadcast_to(found[1][0], (16, 128))
    meta_ref[2] = jnp.broadcast_to(found[0][0] + found[1][0], (16, 128))
    for c in loads:
        c.wait()
    qs_ref[...] = q_ref[...] * jnp.asarray(0.125, BF16)

    pl.semaphore_wait(barrier, 17)

    sent = []

    def copy(src, dst, ss, rs, **to):
        c = pltpu.make_async_remote_copy(
            src_ref=src,
            dst_ref=dst,
            send_sem=ss,
            recv_sem=rs,
            device_id=to,
            device_id_type=MESH,
        )
        c.start()
        sent.append(c)
        return c

    metas = {}
    for d in (1, 3, 2):
        metas["x", d] = copy(
            meta_ref.at[0:2],
            meta_x.at[d - 1],
            meta_ss.at[0, d - 1],
            meta_rs.at[0, d - 1],
            views=view(-d, 0),
        )
        metas["y", d] = copy(
            meta_ref.at[0:2],
            meta_y.at[d - 1],
            meta_ss.at[1, d - 1],
            meta_rs.at[1, d - 1],
            views=view(0, -d),
        )

    own = ((k_ref, v_ref), (qs_ref, g_ref))
    nears = {}

    def send_near(group):
        for arr in range(2):
            for d in (1, 3):
                for half in range(2):
                    nears[group, half, d, arr] = copy(
                        own[group][arr].at[:, half * HALF : (half + 1) * HALF],
                        near.at[group, half, d - 1, arr],
                        near_ss.at[group, half, d - 1, arr],
                        near_rs.at[group, half, d - 1, arr],
                        views=view(d, 0) if half == 0 else view(0, d),
                    )

    passed = {}

    def pass_on(group):
        for arr in range(2):
            for d in (1, 3):
                for half in range(2):
                    nears[group, half, d, arr].wait_recv()
                    rows = slice(0, BLK) if d == 1 else slice(BLK, 2 * BLK)
                    passed[group, half, d, arr] = copy(
                        near.at[group, half, d - 1, arr, rows, :],
                        near.at[group, half, 1, arr, rows, :],
                        near_ss.at[group, half, d, arr],
                        near_rs.at[group, half, d, arr],
                        views=view(d, 0) if half == 0 else view(0, d),
                    )

    wins = {}

    def send_window(group):
        rows = slice(BLK, 2 * BLK) if group == 0 else slice(0, BLK)
        target = kv_in if group == 0 else qg_in
        for arr in range(2):
            for half in range(2):
                wins[group, half, arr] = copy(
                    own[group][arr].at[rows, half * HALF : (half + 1) * HALF],
                    target.at[0, half, arr],
                    win_ss.at[group, half, arr],
                    win_rs.at[group, half, arr],
                    sub=after if group == 0 else ahead,
                )

    send_near(0)
    send_window(0)
    send_window(1)

    lane = lax.broadcasted_iota(jnp.int32, (1, 128), 1)
    low = jnp.where(lane < 64, 1.0, 0.0)
    low16, high16 = low.astype(BF16), (1.0 - low).astype(BF16)

    def stack(piece):
        return jnp.concatenate([piece * low16, piece * high16], axis=0)

    def wide(row):
        return jnp.concatenate([row, row], axis=1)

    def forward(entry, p, qp, gp, kp, vp):
        scores = nt(kp, stack(qp))
        grads = nt(vp, stack(gp))
        top = jnp.max(scores, axis=0, keepdims=True)
        raised = jnp.exp(scores - top)
        raised_buf[entry, p] = raised
        grad_buf[entry, p] = grads
        max_buf[entry, p : p + 1, :] = top
        sum_buf[entry, p : p + 1, :] = jnp.sum(raised, axis=0, keepdims=True)

    def local_forward(n, carry):
        q_rows = pl.ds(pl.multiple_of(jnp.minimum(n, 1) * BLK, BLK), BLK)
        k_rows = pl.ds(pl.multiple_of((n // 2) * BLK, BLK), BLK)
        for p in range(PAIRS):
            cols = slice(p * 128, (p + 1) * 128)
            forward(
                LOCAL + n,
                p,
                qs_ref[q_rows, cols],
                g_ref[q_rows, cols],
                k_ref[k_rows, cols],
                v_ref[k_rows, cols],
            )
        return carry

    lax.fori_loop(0, 3, local_forward, 0)

    for c in metas.values():
        c.wait_recv()

    def meta_of(axis, d, plane, row):
        if d % SIDE == 0:
            got = meta_ref[plane, pl.ds(row, 1), :]
        elif axis == "x":
            got = meta_x[d % SIDE - 1, plane, pl.ds(row, 1), :]
        else:
            got = meta_y[d % SIDE - 1, plane, pl.ds(row, 1), :]
        return got.astype(BF16)

    def want(group, half, j, d):
        if group == 0 and half == 0:
            return meta_of("y", d, 0, view(-j, 0))
        if group == 0:
            return meta_of("x", d, 0, view(0, -j))
        if half == 0:
            return meta_of("x", -j, 1, view(0, d))
        return meta_of("y", -j, 1, view(d, 0))

    fars = {}

    def send_far(group, j):
        if j == 2:
            for c in (passed[group, h, d, r] for h in range(2) for d in (1, 3) for r in range(2)):
                c.wait_recv()
        target = kv_in if group == 0 else qg_in
        for d in (1, 3, 2, 0):
            for half in range(2):
                if d == 0 and j == 0:
                    continue
                slot = j * SIDE + d if half == 0 else d * SIDE + j
                weight = wide(want(group, half, j, d))
                for arr in range(2):
                    if j:
                        first = near[group, half, j - 1, arr, 0:BLK, :]
                        second = near[group, half, j - 1, arr, BLK : 2 * BLK, :]
                    else:
                        cols = slice(half * HALF, (half + 1) * HALF)
                        first = own[group][arr][0:BLK, cols]
                        second = own[group][arr][BLK : 2 * BLK, cols]
                    chosen = pick(first, second, weight)
                    if d:
                        stage[group, half, j, d - 1, arr] = chosen
                    else:
                        target[slot, half, arr] = chosen
                if d:
                    fars[group, half, slot] = copy(
                        stage.at[group, half, j, d - 1],
                        target.at[slot, half],
                        far_ss.at[group, half, j, d - 1],
                        far_rs.at[group, half, j, d - 1],
                        views=view(0, d) if half == 0 else view(d, 0),
                    )

    send_far(0, 0)
    pass_on(0)
    send_far(0, 1)
    send_far(0, 3)
    send_far(0, 2)
    send_near(1)

    def view_of_slot(i):
        return lax.rem(x + SIDE - i // SIDE, SIDE) * SIDE + lax.rem(y + SIDE - i % SIDE, SIDE)

    def slot_of(half, j, n):
        return j * SIDE + n if half == 0 else n * SIDE + j

    def remote_forward(half, j, n):
        i = slot_of(half, j, n)
        weight = meta_ref[1, pl.ds(view_of_slot(i), 1), :].astype(BF16)
        if i == 0:
            weight = weight * 0
        for p in (2 * half, 2 * half + 1):
            cols = slice(p * 128, (p + 1) * 128)
            inner = slice((p % 2) * 128, (p % 2 + 1) * 128)
            forward(
                i,
                p,
                pick(qs_ref[0:BLK, cols], qs_ref[BLK : 2 * BLK, cols], weight),
                pick(g_ref[0:BLK, cols], g_ref[BLK : 2 * BLK, cols], weight),
                kv_in[i, half, 0, :, inner],
                kv_in[i, half, 1, :, inner],
            )

    def wait_items(group, j, n):
        for half in range(2):
            if n:
                fars[group, half, slot_of(half, j, n)].wait_recv()
            elif j == 0:
                for arr in range(2):
                    wins[group, half, arr].wait_recv()

    for j in (0, 1, 3, 2):
        for n in (0, 1, 3, 2):
            wait_items(0, j, n)
            for half in range(2):
                remote_forward(half, j, n)
        if j == 1:
            send_far(1, 0)

    has_prev = jnp.where(band > 0, 1.0, 0.0)
    ones = jnp.full((1, HALF), 1.0, F32)
    uses = []
    for e in range(ENTRIES):
        if e == 0:
            uses.append((ones * has_prev, ones * 0.0))
        elif e < LOCAL:
            row = view(-(e // SIDE), -(e % SIDE))
            second = wide(meta_ref[1, pl.ds(row, 1), :])
            live = wide(meta_ref[2, pl.ds(row, 1), :])
            uses.append((live * (1.0 - second), live * second))
        else:
            second = ones * (0.0 if e == LOCAL else 1.0)
            uses.append((1.0 - second, second))
    tops, invs = [], []
    for blk in range(2):
        top = jnp.full((PAIRS, HALF), -FAR, F32)
        for e in range(ENTRIES):
            top = jnp.maximum(top, max_buf[e] + (uses[e][blk] - 1.0) * FAR)
        tops.append(top)
        total = jnp.zeros((PAIRS, HALF), F32)
        for e in range(ENTRIES):
            total += uses[e][blk] * sum_buf[e] * jnp.exp(jnp.minimum(max_buf[e] - top, 0.0))
        invs.append(1.0 / total)
    for e in range(ENTRIES):
        scale_buf[e] = sum(
            uses[e][blk] * jnp.exp(jnp.minimum(max_buf[e] - tops[blk], 0.0)) * invs[blk]
            for blk in range(2)
        )

    def delta_part(e, carry):
        for p in range(PAIRS):
            prob = raised_buf[e, p] * scale_buf[e, p : p + 1, :]
            rounded = prob.astype(BF16).astype(F32)
            delta_buf[e, p : p + 1, :] = jnp.sum(rounded * grad_buf[e, p], axis=0, keepdims=True)
        return carry

    lax.fori_loop(0, ENTRIES, delta_part, 0)
    deltas = [
        sum(uses[e][blk] * delta_buf[e] for e in range(ENTRIES)) for blk in range(2)
    ]
    stats = {}
    for e in range(ENTRIES):
        first, second = uses[e]
        delta = first * deltas[0] + second * deltas[1]
        delta_buf[e] = delta
        if e < LOCAL:
            a, b = e // SIDE, e % SIDE
            stat_out[e, 0:4, :] = (
                first * tops[0] + second * tops[1] + (1.0 - first - second) * FAR
            )
            stat_out[e, 4:8, :] = first * invs[0] + second * invs[1]
            stat_out[e, 8:12, :] = delta
            if e:
                stat_out[e, 12:16, :] = jnp.broadcast_to(
                    wide(meta_ref[0, pl.ds(view(-a, -b), 1), :]), (4, HALF)
                )
            else:
                stat_out[e, 12:16, :] = jnp.ones((4, HALF), F32)
            slot = (-a % SIDE) * SIDE + (-b % SIDE)
            to = {"views": view(-a, -b)} if e else {"sub": ahead}
            stats[slot] = copy(
                stat_out.at[e], stat_in.at[slot], stat_ss.at[slot], stat_rs.at[slot], **to
            )

    pass_on(1)
    send_far(1, 1)
    send_far(1, 3)

    dq_acc[...] = jnp.zeros_like(dq_acc)
    dk_acc[...] = jnp.zeros_like(dk_acc)
    dv_acc[...] = jnp.zeros_like(dv_acc)

    def score_gradient(e, p):
        prob = raised_buf[e, p] * scale_buf[e, p : p + 1, :]
        return prob, (prob * (grad_buf[e, p] - delta_buf[e, p : p + 1, :])).astype(BF16)

    def halves(both):
        return jnp.where(lane < 64, both[0:BLK, :], both[BLK : 2 * BLK, :])

    def local_backward(n, carry):
        q_rows = pl.ds(pl.multiple_of(jnp.minimum(n, 1) * BLK, BLK), BLK)
        k_rows = pl.ds(pl.multiple_of((n // 2) * BLK, BLK), BLK)
        for p in range(PAIRS):
            cols = slice(p * 128, (p + 1) * 128)
            prob, ds = score_gradient(LOCAL + n, p)
            dq_acc[q_rows, cols] += halves(tn(ds, k_ref[k_rows, cols]))
            dk_acc[k_rows, cols] += nn(ds, stack(qs_ref[q_rows, cols]))
            dv_acc[k_rows, cols] += nn(prob.astype(BF16), stack(g_ref[q_rows, cols]))
        return carry

    lax.fori_loop(0, 3, local_backward, 0)

    def remote_backward(i, carry):
        weight = meta_ref[1, pl.ds(view_of_slot(i), 1), :]
        weight = jnp.where(i == 0, 0.0, weight)
        for p in range(PAIRS):
            cols = slice(p * 128, (p + 1) * 128)
            inner = slice((p % 2) * 128, (p % 2 + 1) * 128)
            _, ds = score_gradient(i, p)
            part = halves(tn(ds, kv_in[i, p // 2, 0, :, inner]))
            dq_acc[0:BLK, cols] += part * (1.0 - weight)
            dq_acc[BLK : 2 * BLK, cols] += part * weight
        return carry

    send_far(1, 2)
    lax.fori_loop(0, LOCAL, remote_backward, 0, unroll=2)
    dq_ref[...] = (dq_acc[...] * 0.125).astype(BF16)

    def owner_backward(half, j, n):
        i = slot_of(half, j, n)
        weight = stat_in[i, 12:13, 0:128]
        weight16 = weight.astype(BF16)
        for p in (2 * half, 2 * half + 1):
            cols = slice(p * 128, (p + 1) * 128)
            inner = slice((p % 2) * 128, (p % 2 + 1) * 128)
            kp = pick(k_ref[0:BLK, cols], k_ref[BLK : 2 * BLK, cols], weight16)
            vp = pick(v_ref[0:BLK, cols], v_ref[BLK : 2 * BLK, cols], weight16)
            qp = stack(qg_in[i, half, 0, :, inner])
            gp = stack(qg_in[i, half, 1, :, inner])
            prob = jnp.exp(nt(kp, qp) - stat_in[i, p : p + 1, :]) * stat_in[i, 4 + p : 5 + p, :]
            ds = (prob * (nt(vp, gp) - stat_in[i, 8 + p : 9 + p, :])).astype(BF16)
            dk = nn(ds, qp)
            dv = nn(prob.astype(BF16), gp)
            dk_acc[0:BLK, cols] += dk * (1.0 - weight)
            dk_acc[BLK : 2 * BLK, cols] += dk * weight
            dv_acc[0:BLK, cols] += dv * (1.0 - weight)
            dv_acc[BLK : 2 * BLK, cols] += dv * weight

    for c in stats.values():
        c.wait_recv()
    for j in (0, 1, 3, 2):
        for n in (0, 1, 3, 2):
            wait_items(1, j, n)
            for half in range(2):
                owner_backward(half, j, n)

    dk_ref[...] = dk_acc[...].astype(BF16)
    dv_ref[...] = dv_acc[...].astype(BF16)
    for c in sent:
        c.wait_send()


def shards(queries, keys, values, out_grad, block_lists):
    vmem = pl.BlockSpec(memory_space=pltpu.VMEM)
    rows = 2 * BLK
    dma = pltpu.SemaphoreType.DMA
    stat_rows = (ENTRIES, PAIRS, HALF)
    return pl.pallas_call(
        kernel,
        out_shape=[pltpu.VMEM((rows, WIDTH), BF16)] * 3,
        in_specs=[vmem] + [pl.BlockSpec(memory_space=pl.ANY)] * 4,
        out_specs=[vmem] * 3,
        scratch_shapes=[
            *[pltpu.VMEM((rows, WIDTH), BF16)] * 5,
            pltpu.VMEM((3, 16, 128), F32),
            pltpu.VMEM((3, 2, 16, 128), F32),
            pltpu.VMEM((3, 2, 16, 128), F32),
            pltpu.VMEM((2, 2, 3, 2, rows, HALF), BF16),
            pltpu.VMEM((2, 2, 4, 3, 2, BLK, HALF), BF16),
            pltpu.VMEM((16, 2, 2, BLK, HALF), BF16),
            pltpu.VMEM((16, 2, 2, BLK, HALF), BF16),
            pltpu.VMEM((ENTRIES, PAIRS, BLK, HALF), F32),
            pltpu.VMEM((ENTRIES, PAIRS, BLK, HALF), F32),
            pltpu.VMEM(stat_rows, F32),
            pltpu.VMEM(stat_rows, F32),
            pltpu.VMEM(stat_rows, F32),
            pltpu.VMEM(stat_rows, F32),
            pltpu.VMEM((16, 16, HALF), F32),
            pltpu.VMEM((16, 16, HALF), F32),
            pltpu.VMEM((rows, WIDTH), F32),
            pltpu.VMEM((rows, WIDTH), F32),
            pltpu.VMEM((rows, WIDTH), F32),
            dma((2, 3)),
            dma((2, 3)),
            dma((2, 2, 4, 2)),
            dma((2, 2, 4, 2)),
            dma((2, 2, 4, 3)),
            dma((2, 2, 4, 3)),
            dma((2, 2, 2)),
            dma((2, 2, 2)),
            dma((16,)),
            dma((16,)),
            dma((4,)),
        ],
        compiler_params=pltpu.CompilerParams(
            collective_id=0, has_side_effects=True, vmem_limit_bytes=60 * 1024 * 1024
        ),
    )(block_lists, queries, keys, values, out_grad)


def solution(mesh):
    spec = P(("views", "sub"), None)
    return jax.shard_map(
        shards,
        mesh=mesh,
        in_specs=(spec,) * 5,
        out_specs=(spec,) * 3,
        check_vma=False,
    )
```

```python
import jax
import jax.numpy as jnp
from jax import lax
from jax.experimental import pallas as pl
from jax.experimental.pallas import tpu as pltpu
from jax.sharding import PartitionSpec as P

MESH = pl.DeviceIdType.MESH
F32 = jnp.float32
BF16 = jnp.bfloat16
SIDE = 4
BLK = 128
WIDTH = 512
HALF = 256
PAIRS = 4
LOCAL = 16
ENTRIES = 19
FAR = 1e30


def nt(a, b):
    return lax.dot_general(a, b, (((1,), (1,)), ((), ())), preferred_element_type=F32)


def nn(a, b):
    return lax.dot_general(a, b, (((1,), (0,)), ((), ())), preferred_element_type=F32)


def tn(a, b):
    return lax.dot_general(a, b, (((0,), (0,)), ((), ())), preferred_element_type=F32)


def pick(first, second, second_weight):
    return first * (1 - second_weight) + second * second_weight


def kernel(
    lists_ref,
    q_hbm,
    k_hbm,
    v_hbm,
    g_hbm,
    dq_ref,
    dk_ref,
    dv_ref,
    q_ref,
    k_ref,
    v_ref,
    g_ref,
    qs_ref,
    meta_ref,
    meta_x,
    meta_y,
    block_out,
    block_in,
    near,
    stage,
    kv_in,
    qg_in,
    raised_buf,
    grad_buf,
    max_buf,
    sum_buf,
    scale_buf,
    delta_buf,
    stat_out,
    stat_in,
    dq_acc,
    dk_acc,
    dv_acc,
    meta_ss,
    meta_rs,
    near_ss,
    near_rs,
    far_ss,
    far_rs,
    win_ss,
    win_rs,
    stat_ss,
    stat_rs,
    load_sem,
    block_ss,
    block_rs,
):
    loads = []
    for n, (src, dst) in enumerate(
        ((k_hbm, k_ref), (v_hbm, v_ref), (q_hbm, q_ref), (g_hbm, g_ref))
    ):
        loads.append(pltpu.make_async_copy(src, dst, load_sem.at[n]))
        loads[n].start()
    me = lax.axis_index("views")
    band = lax.axis_index("sub")
    bands = lax.axis_size("sub")
    x, y = me // SIDE, me % SIDE
    after = lax.rem(band + 1, bands)
    ahead = lax.rem(band + bands - 1, bands)

    def view(a, b):
        return lax.rem(x + (a % SIDE), SIDE) * SIDE + lax.rem(y + (b % SIDE), SIDE)


    barrier = pltpu.get_barrier_semaphore()
    for d in (1, 3, 2):
        for peer in (view(d, 0), view(0, d)):
            pl.semaphore_signal(
                barrier, inc=1, device_id={"views": peer}, device_id_type=MESH
            )
    for s in (after, ahead):
        pl.semaphore_signal(barrier, inc=1, device_id={"sub": s}, device_id_type=MESH)

    lists = lists_ref[...]
    views = lax.broadcasted_iota(jnp.int32, (16, 16), 0)
    found = []
    for row in range(2):
        ids = jnp.broadcast_to(lists[row : row + 1, :], (16, 16))
        hit = (ids >= 0) & ((ids >> 4) == views)
        live = jnp.sum(jnp.where(hit, 1.0, 0.0), axis=1, keepdims=True)
        odd = jnp.sum(jnp.where(hit & ((ids & 1) == 1), 1.0, 0.0), axis=1, keepdims=True)
        found.append((live, odd))
    meta_ref[0] = jnp.broadcast_to(found[0][1] + found[1][1], (16, 128))
    meta_ref[1] = jnp.broadcast_to(found[1][0], (16, 128))
    meta_ref[2] = jnp.broadcast_to(found[0][0] + found[1][0], (16, 128))
    for c in loads:
        c.wait()
    qs_ref[...] = q_ref[...] * jnp.asarray(0.125, BF16)

    pl.semaphore_wait(barrier, 8)

    sent = []

    def copy(src, dst, ss, rs, **to):
        c = pltpu.make_async_remote_copy(
            src_ref=src,
            dst_ref=dst,
            send_sem=ss,
            recv_sem=rs,
            device_id=to,
            device_id_type=MESH,
        )
        c.start()
        sent.append(c)
        return c

    metas = {}
    for d in (1, 3, 2):
        metas["x", d] = copy(
            meta_ref.at[0:2],
            meta_x.at[d - 1],
            meta_ss.at[0, d - 1],
            meta_rs.at[0, d - 1],
            views=view(-d, 0),
        )
        metas["y", d] = copy(
            meta_ref.at[0:2],
            meta_y.at[d - 1],
            meta_ss.at[1, d - 1],
            meta_rs.at[1, d - 1],
            views=view(0, -d),
        )

    own = ((k_ref, v_ref), (qs_ref, g_ref))
    nears = {}

    def send_near(group):
        for arr in range(2):
            for d in (1, 3):
                for half in range(2):
                    nears[group, half, d, arr] = copy(
                        own[group][arr].at[:, half * HALF : (half + 1) * HALF],
                        near.at[group, half, d - 1, arr],
                        near_ss.at[group, half, d - 1, arr],
                        near_rs.at[group, half, d - 1, arr],
                        views=view(d, 0) if half == 0 else view(0, d),
                    )

    passed = {}

    def pass_on(group):
        for arr in range(2):
            for d in (1, 3):
                for half in range(2):
                    nears[group, half, d, arr].wait_recv()
                    rows = slice(0, BLK) if d == 1 else slice(BLK, 2 * BLK)
                    passed[group, half, d, arr] = copy(
                        near.at[group, half, d - 1, arr, rows, :],
                        near.at[group, half, 1, arr, rows, :],
                        near_ss.at[group, half, d, arr],
                        near_rs.at[group, half, d, arr],
                        views=view(d, 0) if half == 0 else view(0, d),
                    )

    wins = {}

    def send_window(group):
        rows = slice(BLK, 2 * BLK) if group == 0 else slice(0, BLK)
        target = kv_in if group == 0 else qg_in
        for arr in range(2):
            for half in range(2):
                wins[group, half, arr] = copy(
                    own[group][arr].at[rows, half * HALF : (half + 1) * HALF],
                    target.at[0, half, arr],
                    win_ss.at[group, half, arr],
                    win_rs.at[group, half, arr],
                    sub=after if group == 0 else ahead,
                )

    send_near(0)
    send_window(0)
    send_window(1)

    lane = lax.broadcasted_iota(jnp.int32, (1, 128), 1)
    low = jnp.where(lane < 64, 1.0, 0.0)
    low16, high16 = low.astype(BF16), (1.0 - low).astype(BF16)

    def stack(piece):
        return jnp.concatenate([piece * low16, piece * high16], axis=0)

    def wide(row):
        return jnp.concatenate([row, row], axis=1)

    def forward(entry, p, qp, gp, kp, vp):
        scores = nt(kp, stack(qp))
        grads = nt(vp, stack(gp))
        top = jnp.max(scores, axis=0, keepdims=True)
        raised = jnp.exp(scores - top)
        raised_buf[entry, p] = raised
        grad_buf[entry, p] = grads
        max_buf[entry, p : p + 1, :] = top
        sum_buf[entry, p : p + 1, :] = jnp.sum(raised, axis=0, keepdims=True)

    def local_forward(n, carry):
        q_rows = pl.ds(pl.multiple_of(jnp.minimum(n, 1) * BLK, BLK), BLK)
        k_rows = pl.ds(pl.multiple_of((n // 2) * BLK, BLK), BLK)
        for p in range(PAIRS):
            cols = slice(p * 128, (p + 1) * 128)
            forward(
                LOCAL + n,
                p,
                qs_ref[q_rows, cols],
                g_ref[q_rows, cols],
                k_ref[k_rows, cols],
                v_ref[k_rows, cols],
            )
        return carry

    lax.fori_loop(0, 3, local_forward, 0)

    for c in metas.values():
        c.wait_recv()

    def meta_of(axis, d, plane, row):
        if d % SIDE == 0:
            got = meta_ref[plane, pl.ds(row, 1), :]
        elif axis == "x":
            got = meta_x[d % SIDE - 1, plane, pl.ds(row, 1), :]
        else:
            got = meta_y[d % SIDE - 1, plane, pl.ds(row, 1), :]
        return got

    blocks = {}
    for d in (1, 3, 2):
        for a in range(SIDE):
            block_out[d - 1, a : a + 1, :] = meta_of("x", -a, 0, view(0, d))
        block_out[d - 1, 4:8, :] = jnp.zeros((4, 128), F32)
        blocks[d] = copy(
            block_out.at[d - 1],
            block_in.at[d - 1],
            block_ss.at[d - 1],
            block_rs.at[d - 1],
            views=view(0, d),
        )

    def want(group, half, j, d):
        if group == 0 and half == 0:
            return meta_of("y", d, 0, view(-j, 0))
        if group == 0:
            return meta_of("x", d, 0, view(0, -j))
        if half == 0:
            return meta_of("x", -j, 1, view(0, d))
        return meta_of("y", -j, 1, view(d, 0))

    fars = {}

    def send_far(group, j):
        if j == 2:
            for c in (passed[group, h, d, r] for h in range(2) for d in (1, 3) for r in range(2)):
                c.wait_recv()
        target = kv_in if group == 0 else qg_in
        for d in (1, 3, 2, 0):
            for half in range(2):
                if d == 0 and j == 0:
                    continue
                slot = j * SIDE + d if half == 0 else d * SIDE + j
                weight = wide(want(group, half, j, d).astype(BF16))
                for arr in range(2):
                    if j:
                        first = near[group, half, j - 1, arr, 0:BLK, :]
                        second = near[group, half, j - 1, arr, BLK : 2 * BLK, :]
                    else:
                        cols = slice(half * HALF, (half + 1) * HALF)
                        first = own[group][arr][0:BLK, cols]
                        second = own[group][arr][BLK : 2 * BLK, cols]
                    chosen = pick(first, second, weight)
                    if d:
                        stage[group, half, j, d - 1, arr] = chosen
                    else:
                        target[slot, half, arr] = chosen
                if d:
                    fars[group, half, slot] = copy(
                        stage.at[group, half, j, d - 1],
                        target.at[slot, half],
                        far_ss.at[group, half, j, d - 1],
                        far_rs.at[group, half, j, d - 1],
                        views=view(0, d) if half == 0 else view(d, 0),
                    )

    send_far(0, 0)
    pass_on(0)
    send_far(0, 1)
    send_far(0, 3)
    send_far(0, 2)
    send_near(1)

    def view_of_slot(i):
        return lax.rem(x + SIDE - i // SIDE, SIDE) * SIDE + lax.rem(y + SIDE - i % SIDE, SIDE)

    def slot_of(half, j, n):
        return j * SIDE + n if half == 0 else n * SIDE + j

    def remote_forward(half, j, n):
        i = slot_of(half, j, n)
        weight = meta_ref[1, pl.ds(view_of_slot(i), 1), :].astype(BF16)
        if i == 0:
            weight = weight * 0
        for p in (2 * half, 2 * half + 1):
            cols = slice(p * 128, (p + 1) * 128)
            inner = slice((p % 2) * 128, (p % 2 + 1) * 128)
            forward(
                i,
                p,
                pick(qs_ref[0:BLK, cols], qs_ref[BLK : 2 * BLK, cols], weight),
                pick(g_ref[0:BLK, cols], g_ref[BLK : 2 * BLK, cols], weight),
                kv_in[i, half, 0, :, inner],
                kv_in[i, half, 1, :, inner],
            )

    def wait_items(group, j, n):
        for half in range(2):
            if n:
                fars[group, half, slot_of(half, j, n)].wait_recv()
            elif j == 0:
                for arr in range(2):
                    wins[group, half, arr].wait_recv()

    for j in (0, 1, 3, 2):
        for n in (0, 1, 3, 2):
            wait_items(0, j, n)
            for half in range(2):
                remote_forward(half, j, n)
        if j == 1:
            send_far(1, 0)

    has_prev = jnp.where(band > 0, 1.0, 0.0)
    ones = jnp.full((1, HALF), 1.0, F32)
    uses = []
    for e in range(ENTRIES):
        if e == 0:
            uses.append((ones * has_prev, ones * 0.0))
        elif e < LOCAL:
            row = view(-(e // SIDE), -(e % SIDE))
            second = wide(meta_ref[1, pl.ds(row, 1), :])
            live = wide(meta_ref[2, pl.ds(row, 1), :])
            uses.append((live * (1.0 - second), live * second))
        else:
            second = ones * (0.0 if e == LOCAL else 1.0)
            uses.append((1.0 - second, second))
    tops, invs = [], []
    for blk in range(2):
        top = jnp.full((PAIRS, HALF), -FAR, F32)
        for e in range(ENTRIES):
            top = jnp.maximum(top, max_buf[e] + (uses[e][blk] - 1.0) * FAR)
        tops.append(top)
        total = jnp.zeros((PAIRS, HALF), F32)
        for e in range(ENTRIES):
            total += uses[e][blk] * sum_buf[e] * jnp.exp(jnp.minimum(max_buf[e] - top, 0.0))
        invs.append(1.0 / total)
    for e in range(ENTRIES):
        scale_buf[e] = sum(
            uses[e][blk] * jnp.exp(jnp.minimum(max_buf[e] - tops[blk], 0.0)) * invs[blk]
            for blk in range(2)
        )

    def delta_part(e, carry):
        for p in range(PAIRS):
            prob = raised_buf[e, p] * scale_buf[e, p : p + 1, :]
            rounded = prob.astype(BF16).astype(F32)
            delta_buf[e, p : p + 1, :] = jnp.sum(rounded * grad_buf[e, p], axis=0, keepdims=True)
        return carry

    lax.fori_loop(0, ENTRIES, delta_part, 0)
    deltas = [
        sum(uses[e][blk] * delta_buf[e] for e in range(ENTRIES)) for blk in range(2)
    ]
    logs = [tops[blk] - jnp.log(invs[blk]) for blk in range(2)]
    stats = {}
    for e in range(ENTRIES):
        first, second = uses[e]
        delta = first * deltas[0] + second * deltas[1]
        delta_buf[e] = delta
        if e < LOCAL:
            a, b = e // SIDE, e % SIDE
            stat_out[e, 0:4, :] = first * logs[0] + second * logs[1] + (1.0 - first - second) * FAR
            stat_out[e, 4:8, :] = delta
            slot = (-a % SIDE) * SIDE + (-b % SIDE)
            to = {"views": view(-a, -b)} if e else {"sub": ahead}
            stats[slot] = copy(
                stat_out.at[e], stat_in.at[slot], stat_ss.at[slot], stat_rs.at[slot], **to
            )

    pass_on(1)
    send_far(1, 1)
    send_far(1, 3)

    dq_acc[...] = jnp.zeros_like(dq_acc)
    dk_acc[...] = jnp.zeros_like(dk_acc)
    dv_acc[...] = jnp.zeros_like(dv_acc)

    def score_gradient(e, p):
        prob = raised_buf[e, p] * scale_buf[e, p : p + 1, :]
        return prob, (prob * (grad_buf[e, p] - delta_buf[e, p : p + 1, :])).astype(BF16)

    def halves(both):
        return jnp.where(lane < 64, both[0:BLK, :], both[BLK : 2 * BLK, :])

    def local_backward(n, carry):
        q_rows = pl.ds(pl.multiple_of(jnp.minimum(n, 1) * BLK, BLK), BLK)
        k_rows = pl.ds(pl.multiple_of((n // 2) * BLK, BLK), BLK)
        for p in range(PAIRS):
            cols = slice(p * 128, (p + 1) * 128)
            prob, ds = score_gradient(LOCAL + n, p)
            dq_acc[q_rows, cols] += halves(tn(ds, k_ref[k_rows, cols]))
            dk_acc[k_rows, cols] += nn(ds, stack(qs_ref[q_rows, cols]))
            dv_acc[k_rows, cols] += nn(prob.astype(BF16), stack(g_ref[q_rows, cols]))
        return carry

    lax.fori_loop(0, 3, local_backward, 0)

    def remote_backward(i, carry):
        weight = meta_ref[1, pl.ds(view_of_slot(i), 1), :]
        weight = jnp.where(i == 0, 0.0, weight)
        for p in range(PAIRS):
            cols = slice(p * 128, (p + 1) * 128)
            inner = slice((p % 2) * 128, (p % 2 + 1) * 128)
            _, ds = score_gradient(i, p)
            part = halves(tn(ds, kv_in[i, p // 2, 0, :, inner]))
            dq_acc[0:BLK, cols] += part * (1.0 - weight)
            dq_acc[BLK : 2 * BLK, cols] += part * weight
        return carry

    send_far(1, 2)
    lax.fori_loop(0, LOCAL, remote_backward, 0, unroll=2)
    dq_ref[...] = (dq_acc[...] * 0.125).astype(BF16)

    def owner_backward(half, j, n):
        i = slot_of(half, j, n)
        a, b = i // SIDE, i % SIDE
        if i == 0:
            weight = jnp.ones((1, 128), F32)
        elif b == 0:
            weight = meta_of("x", -a, 0, me)
        else:
            weight = block_in[b - 1, a : a + 1, :]
        weight16 = weight.astype(BF16)
        for p in (2 * half, 2 * half + 1):
            cols = slice(p * 128, (p + 1) * 128)
            inner = slice((p % 2) * 128, (p % 2 + 1) * 128)
            kp = pick(k_ref[0:BLK, cols], k_ref[BLK : 2 * BLK, cols], weight16)
            vp = pick(v_ref[0:BLK, cols], v_ref[BLK : 2 * BLK, cols], weight16)
            qp = stack(qg_in[i, half, 0, :, inner])
            gp = stack(qg_in[i, half, 1, :, inner])
            prob = jnp.exp(nt(kp, qp) - stat_in[i, p : p + 1, :])
            ds = (prob * (nt(vp, gp) - stat_in[i, 4 + p : 5 + p, :])).astype(BF16)
            dk = nn(ds, qp)
            dv = nn(prob.astype(BF16), gp)
            dk_acc[0:BLK, cols] += dk * (1.0 - weight)
            dk_acc[BLK : 2 * BLK, cols] += dk * weight
            dv_acc[0:BLK, cols] += dv * (1.0 - weight)
            dv_acc[BLK : 2 * BLK, cols] += dv * weight

    for c in (*blocks.values(), *stats.values()):
        c.wait_recv()
    for j in (0, 1, 3, 2):
        for n in (0, 1, 3, 2):
            wait_items(1, j, n)
            for half in range(2):
                owner_backward(half, j, n)

    dk_ref[...] = dk_acc[...].astype(BF16)
    dv_ref[...] = dv_acc[...].astype(BF16)
    for c in sent:
        c.wait_send()


def shards(queries, keys, values, out_grad, block_lists):
    vmem = pl.BlockSpec(memory_space=pltpu.VMEM)
    rows = 2 * BLK
    dma = pltpu.SemaphoreType.DMA
    stat_rows = (ENTRIES, PAIRS, HALF)
    return pl.pallas_call(
        kernel,
        out_shape=[pltpu.VMEM((rows, WIDTH), BF16)] * 3,
        in_specs=[vmem] + [pl.BlockSpec(memory_space=pl.ANY)] * 4,
        out_specs=[vmem] * 3,
        scratch_shapes=[
            *[pltpu.VMEM((rows, WIDTH), BF16)] * 5,
            pltpu.VMEM((3, 16, 128), F32),
            pltpu.VMEM((3, 2, 16, 128), F32),
            pltpu.VMEM((3, 2, 16, 128), F32),
            pltpu.VMEM((3, 8, 128), F32),
            pltpu.VMEM((3, 8, 128), F32),
            pltpu.VMEM((2, 2, 3, 2, rows, HALF), BF16),
            pltpu.VMEM((2, 2, 4, 3, 2, BLK, HALF), BF16),
            pltpu.VMEM((16, 2, 2, BLK, HALF), BF16),
            pltpu.VMEM((16, 2, 2, BLK, HALF), BF16),
            pltpu.VMEM((ENTRIES, PAIRS, BLK, HALF), F32),
            pltpu.VMEM((ENTRIES, PAIRS, BLK, HALF), F32),
            pltpu.VMEM(stat_rows, F32),
            pltpu.VMEM(stat_rows, F32),
            pltpu.VMEM(stat_rows, F32),
            pltpu.VMEM(stat_rows, F32),
            pltpu.VMEM((16, 8, HALF), F32),
            pltpu.VMEM((16, 8, HALF), F32),
            pltpu.VMEM((rows, WIDTH), F32),
            pltpu.VMEM((rows, WIDTH), F32),
            pltpu.VMEM((rows, WIDTH), F32),
            dma((2, 3)),
            dma((2, 3)),
            dma((2, 2, 4, 2)),
            dma((2, 2, 4, 2)),
            dma((2, 2, 4, 3)),
            dma((2, 2, 4, 3)),
            dma((2, 2, 2)),
            dma((2, 2, 2)),
            dma((16,)),
            dma((16,)),
            dma((4,)),
            dma((3,)),
            dma((3,)),
        ],
        compiler_params=pltpu.CompilerParams(
            collective_id=0, has_side_effects=True, vmem_limit_bytes=60 * 1024 * 1024
        ),
    )(block_lists, queries, keys, values, out_grad)


def solution(mesh):
    spec = P(("views", "sub"), None)
    return jax.shard_map(
        shards,
        mesh=mesh,
        in_specs=(spec,) * 5,
        out_specs=(spec,) * 3,
        check_vma=False,
    )
```

```python
import jax
import jax.numpy as jnp
from jax import lax
from jax.experimental import pallas as pl
from jax.experimental.pallas import tpu as pltpu
from jax.sharding import PartitionSpec as P

MESH = pl.DeviceIdType.MESH
F32 = jnp.float32
BF16 = jnp.bfloat16
SIDE = 4
BLK = 128
WIDTH = 512
HALF = 256
PAIRS = 4
LOCAL = 16
ENTRIES = 19
FAR = 1e30


def nt(a, b):
    return lax.dot_general(a, b, (((1,), (1,)), ((), ())), preferred_element_type=F32)


def nn(a, b):
    return lax.dot_general(a, b, (((1,), (0,)), ((), ())), preferred_element_type=F32)


def tn(a, b):
    return lax.dot_general(a, b, (((0,), (0,)), ((), ())), preferred_element_type=F32)


def pick(first, second, second_weight):
    return first * (1 - second_weight) + second * second_weight


def kernel(
    lists_hbm,
    q_hbm,
    k_hbm,
    v_hbm,
    g_hbm,
    dq_ref,
    dk_ref,
    dv_ref,
    lists_ref,
    q_ref,
    k_ref,
    v_ref,
    g_ref,
    qs_ref,
    meta_ref,
    meta_x,
    meta_y,
    block_out,
    block_in,
    near,
    stage,
    kv_in,
    qg_in,
    raised_buf,
    grad_buf,
    max_buf,
    sum_buf,
    scale_buf,
    delta_buf,
    stat_out,
    stat_in,
    dq_acc,
    dk_acc,
    dv_acc,
    meta_ss,
    meta_rs,
    near_ss,
    near_rs,
    far_ss,
    far_rs,
    win_ss,
    win_rs,
    stat_ss,
    stat_rs,
    load_sem,
    block_ss,
    block_rs,
):
    loads = []
    for n, (src, dst) in enumerate(
        (
            (lists_hbm, lists_ref),
            (k_hbm, k_ref),
            (v_hbm, v_ref),
            (q_hbm, q_ref),
            (g_hbm, g_ref),
        )
    ):
        loads.append(pltpu.make_async_copy(src, dst, load_sem.at[n]))
        loads[n].start()
    me = lax.axis_index("views")
    band = lax.axis_index("sub")
    bands = lax.axis_size("sub")
    x, y = me // SIDE, me % SIDE
    after = lax.rem(band + 1, bands)
    ahead = lax.rem(band + bands - 1, bands)

    def view(a, b):
        return lax.rem(x + (a % SIDE), SIDE) * SIDE + lax.rem(y + (b % SIDE), SIDE)

    barrier = pltpu.get_barrier_semaphore()
    for d in (1, 3, 2):
        for peer in (view(d, 0), view(0, d)):
            pl.semaphore_signal(
                barrier, inc=1, device_id={"views": peer}, device_id_type=MESH
            )
    for s in (after, ahead):
        pl.semaphore_signal(barrier, inc=1, device_id={"sub": s}, device_id_type=MESH)

    loads[0].wait()
    lists = lists_ref[...]
    views = lax.broadcasted_iota(jnp.int32, (16, 16), 0)
    found = []
    for row in range(2):
        ids = jnp.broadcast_to(lists[row : row + 1, :], (16, 16))
        hit = (ids >= 0) & ((ids >> 4) == views)
        live = jnp.sum(jnp.where(hit, 1.0, 0.0), axis=1, keepdims=True)
        odd = jnp.sum(jnp.where(hit & ((ids & 1) == 1), 1.0, 0.0), axis=1, keepdims=True)
        found.append((live, odd))
    meta_ref[0] = jnp.broadcast_to(found[0][1] + found[1][1], (16, 128))
    meta_ref[1] = jnp.broadcast_to(found[1][0], (16, 128))
    meta_ref[2] = jnp.broadcast_to(found[0][0] + found[1][0], (16, 128))
    for c in loads[1:]:
        c.wait()
    qs_ref[...] = q_ref[...] * jnp.asarray(0.125, BF16)

    pl.semaphore_wait(barrier, 8)

    sent = []

    def copy(src, dst, ss, rs, **to):
        c = pltpu.make_async_remote_copy(
            src_ref=src,
            dst_ref=dst,
            send_sem=ss,
            recv_sem=rs,
            device_id=to,
            device_id_type=MESH,
        )
        c.start()
        sent.append(c)
        return c

    metas = {}
    for d in (1, 3, 2):
        metas["x", d] = copy(
            meta_ref.at[0:2],
            meta_x.at[d - 1],
            meta_ss.at[0, d - 1],
            meta_rs.at[0, d - 1],
            views=view(-d, 0),
        )
        metas["y", d] = copy(
            meta_ref.at[0:2],
            meta_y.at[d - 1],
            meta_ss.at[1, d - 1],
            meta_rs.at[1, d - 1],
            views=view(0, -d),
        )

    own = ((k_ref, v_ref), (qs_ref, g_ref))
    nears = {}

    def send_near(group):
        for arr in range(2):
            for d in (1, 3):
                for half in range(2):
                    nears[group, half, d, arr] = copy(
                        own[group][arr].at[:, half * HALF : (half + 1) * HALF],
                        near.at[group, half, d - 1, arr],
                        near_ss.at[group, half, d - 1, arr],
                        near_rs.at[group, half, d - 1, arr],
                        views=view(d, 0) if half == 0 else view(0, d),
                    )

    passed = {}

    def pass_on(group):
        for arr in range(2):
            for d in (1, 3):
                for half in range(2):
                    nears[group, half, d, arr].wait_recv()
                    rows = slice(0, BLK) if d == 1 else slice(BLK, 2 * BLK)
                    passed[group, half, d, arr] = copy(
                        near.at[group, half, d - 1, arr, rows, :],
                        near.at[group, half, 1, arr, rows, :],
                        near_ss.at[group, half, d, arr],
                        near_rs.at[group, half, d, arr],
                        views=view(d, 0) if half == 0 else view(0, d),
                    )

    wins = {}

    def send_window(group):
        rows = slice(BLK, 2 * BLK) if group == 0 else slice(0, BLK)
        target = kv_in if group == 0 else qg_in
        for arr in range(2):
            for half in range(2):
                wins[group, half, arr] = copy(
                    own[group][arr].at[rows, half * HALF : (half + 1) * HALF],
                    target.at[0, half, arr],
                    win_ss.at[group, half, arr],
                    win_rs.at[group, half, arr],
                    sub=after if group == 0 else ahead,
                )

    send_near(0)
    send_window(0)
    send_window(1)

    lane = lax.broadcasted_iota(jnp.int32, (1, 128), 1)
    low = jnp.where(lane < 64, 1.0, 0.0)
    low16, high16 = low.astype(BF16), (1.0 - low).astype(BF16)

    def stack(piece):
        return jnp.concatenate([piece * low16, piece * high16], axis=0)

    def wide(row):
        return jnp.concatenate([row, row], axis=1)

    def forward(entry, p, qp, gp, kp, vp):
        scores = nt(kp, stack(qp))
        grads = nt(vp, stack(gp))
        top = jnp.max(scores, axis=0, keepdims=True)
        raised = jnp.exp(scores - top)
        raised_buf[entry, p] = raised
        grad_buf[entry, p] = grads
        max_buf[entry, p : p + 1, :] = top
        sum_buf[entry, p : p + 1, :] = jnp.sum(raised, axis=0, keepdims=True)

    def local_forward(n, carry):
        q_rows = pl.ds(pl.multiple_of(jnp.minimum(n, 1) * BLK, BLK), BLK)
        k_rows = pl.ds(pl.multiple_of((n // 2) * BLK, BLK), BLK)
        for p in range(PAIRS):
            cols = slice(p * 128, (p + 1) * 128)
            forward(
                LOCAL + n,
                p,
                qs_ref[q_rows, cols],
                g_ref[q_rows, cols],
                k_ref[k_rows, cols],
                v_ref[k_rows, cols],
            )
        return carry

    for c in metas.values():
        c.wait_recv()

    def meta_of(axis, d, plane, row):
        if d % SIDE == 0:
            got = meta_ref[plane, pl.ds(row, 1), :]
        elif axis == "x":
            got = meta_x[d % SIDE - 1, plane, pl.ds(row, 1), :]
        else:
            got = meta_y[d % SIDE - 1, plane, pl.ds(row, 1), :]
        return got

    blocks = {}
    for d in (1, 3, 2):
        for a in range(SIDE):
            block_out[d - 1, a : a + 1, :] = meta_of("x", -a, 0, view(0, d))
        block_out[d - 1, 4:8, :] = jnp.zeros((4, 128), F32)
        blocks[d] = copy(
            block_out.at[d - 1],
            block_in.at[d - 1],
            block_ss.at[d - 1],
            block_rs.at[d - 1],
            views=view(0, d),
        )

    def want(group, half, j, d):
        if group == 0 and half == 0:
            return meta_of("y", d, 0, view(-j, 0))
        if group == 0:
            return meta_of("x", d, 0, view(0, -j))
        if half == 0:
            return meta_of("x", -j, 1, view(0, d))
        return meta_of("y", -j, 1, view(d, 0))

    fars = {}

    def send_far(group, j):
        if j == 2:
            for c in (passed[group, h, d, r] for h in range(2) for d in (1, 3) for r in range(2)):
                c.wait_recv()
        target = kv_in if group == 0 else qg_in
        for d in (1, 3, 2, 0):
            for half in range(2):
                if d == 0 and j == 0:
                    continue
                slot = j * SIDE + d if half == 0 else d * SIDE + j
                weight = wide(want(group, half, j, d).astype(BF16))
                for arr in range(2):
                    if j:
                        first = near[group, half, j - 1, arr, 0:BLK, :]
                        second = near[group, half, j - 1, arr, BLK : 2 * BLK, :]
                    else:
                        cols = slice(half * HALF, (half + 1) * HALF)
                        first = own[group][arr][0:BLK, cols]
                        second = own[group][arr][BLK : 2 * BLK, cols]
                    chosen = pick(first, second, weight)
                    if d:
                        stage[group, half, j, d - 1, arr] = chosen
                    else:
                        target[slot, half, arr] = chosen
                if d:
                    fars[group, half, slot] = copy(
                        stage.at[group, half, j, d - 1],
                        target.at[slot, half],
                        far_ss.at[group, half, j, d - 1],
                        far_rs.at[group, half, j, d - 1],
                        views=view(0, d) if half == 0 else view(d, 0),
                    )

    send_far(0, 0)
    lax.fori_loop(0, 3, local_forward, 0)
    pass_on(0)
    send_far(0, 1)
    send_far(0, 3)
    send_far(0, 2)
    send_near(1)

    def view_of_slot(i):
        return lax.rem(x + SIDE - i // SIDE, SIDE) * SIDE + lax.rem(y + SIDE - i % SIDE, SIDE)

    def slot_of(half, j, n):
        return j * SIDE + n if half == 0 else n * SIDE + j

    def remote_forward(half, j, n):
        i = slot_of(half, j, n)
        weight = meta_ref[1, pl.ds(view_of_slot(i), 1), :].astype(BF16)
        if i == 0:
            weight = weight * 0
        for p in (2 * half, 2 * half + 1):
            cols = slice(p * 128, (p + 1) * 128)
            inner = slice((p % 2) * 128, (p % 2 + 1) * 128)
            forward(
                i,
                p,
                pick(qs_ref[0:BLK, cols], qs_ref[BLK : 2 * BLK, cols], weight),
                pick(g_ref[0:BLK, cols], g_ref[BLK : 2 * BLK, cols], weight),
                kv_in[i, half, 0, :, inner],
                kv_in[i, half, 1, :, inner],
            )

    def wait_items(group, j, n):
        for half in range(2):
            if n:
                fars[group, half, slot_of(half, j, n)].wait_recv()
            elif j == 0:
                for arr in range(2):
                    wins[group, half, arr].wait_recv()

    for j in (0, 1, 3, 2):
        for n in (0, 1, 3, 2):
            wait_items(0, j, n)
            for half in range(2):
                remote_forward(half, j, n)
        if j == 1:
            send_far(1, 0)

    has_prev = jnp.where(band > 0, 1.0, 0.0)
    ones = jnp.full((1, HALF), 1.0, F32)
    uses = []
    for e in range(ENTRIES):
        if e == 0:
            uses.append((ones * has_prev, ones * 0.0))
        elif e < LOCAL:
            row = view(-(e // SIDE), -(e % SIDE))
            second = wide(meta_ref[1, pl.ds(row, 1), :])
            live = wide(meta_ref[2, pl.ds(row, 1), :])
            uses.append((live * (1.0 - second), live * second))
        else:
            second = ones * (0.0 if e == LOCAL else 1.0)
            uses.append((1.0 - second, second))
    tops, invs = [], []
    for blk in range(2):
        top = jnp.full((PAIRS, HALF), -FAR, F32)
        for e in range(ENTRIES):
            top = jnp.maximum(top, max_buf[e] + (uses[e][blk] - 1.0) * FAR)
        tops.append(top)
        total = jnp.zeros((PAIRS, HALF), F32)
        for e in range(ENTRIES):
            total += uses[e][blk] * sum_buf[e] * jnp.exp(jnp.minimum(max_buf[e] - top, 0.0))
        invs.append(1.0 / total)
    for e in range(ENTRIES):
        scale_buf[e] = sum(
            uses[e][blk] * jnp.exp(jnp.minimum(max_buf[e] - tops[blk], 0.0)) * invs[blk]
            for blk in range(2)
        )

    def delta_part(e, carry):
        for p in range(PAIRS):
            prob = raised_buf[e, p] * scale_buf[e, p : p + 1, :]
            rounded = prob.astype(BF16).astype(F32)
            delta_buf[e, p : p + 1, :] = jnp.sum(rounded * grad_buf[e, p], axis=0, keepdims=True)
        return carry

    lax.fori_loop(0, LOCAL, delta_part, 0, unroll=4)
    lax.fori_loop(LOCAL, ENTRIES, delta_part, 0, unroll=3)
    deltas = [
        sum(uses[e][blk] * delta_buf[e] for e in range(ENTRIES)) for blk in range(2)
    ]
    logs = [tops[blk] - jnp.log(invs[blk]) for blk in range(2)]
    stats = {}
    for e in range(ENTRIES):
        first, second = uses[e]
        delta = first * deltas[0] + second * deltas[1]
        delta_buf[e] = delta
        if e < LOCAL:
            a, b = e // SIDE, e % SIDE
            stat_out[e, 0:4, :] = first * logs[0] + second * logs[1] + (1.0 - first - second) * FAR
            stat_out[e, 4:8, :] = delta
            slot = (-a % SIDE) * SIDE + (-b % SIDE)
            to = {"views": view(-a, -b)} if e else {"sub": ahead}
            stats[slot] = copy(
                stat_out.at[e], stat_in.at[slot], stat_ss.at[slot], stat_rs.at[slot], **to
            )

    pass_on(1)
    send_far(1, 1)
    send_far(1, 3)

    dq_acc[...] = jnp.zeros_like(dq_acc)
    dk_acc[...] = jnp.zeros_like(dk_acc)
    dv_acc[...] = jnp.zeros_like(dv_acc)

    def score_gradient(e, p):
        prob = raised_buf[e, p] * scale_buf[e, p : p + 1, :]
        return prob, (prob * (grad_buf[e, p] - delta_buf[e, p : p + 1, :])).astype(BF16)

    def halves(both):
        return jnp.where(lane < 64, both[0:BLK, :], both[BLK : 2 * BLK, :])

    def local_backward(n, carry):
        q_rows = pl.ds(pl.multiple_of(jnp.minimum(n, 1) * BLK, BLK), BLK)
        k_rows = pl.ds(pl.multiple_of((n // 2) * BLK, BLK), BLK)
        for p in range(PAIRS):
            cols = slice(p * 128, (p + 1) * 128)
            prob, ds = score_gradient(LOCAL + n, p)
            dq_acc[q_rows, cols] += halves(tn(ds, k_ref[k_rows, cols]))
            dk_acc[k_rows, cols] += nn(ds, stack(qs_ref[q_rows, cols]))
            dv_acc[k_rows, cols] += nn(prob.astype(BF16), stack(g_ref[q_rows, cols]))
        return carry

    lax.fori_loop(0, 3, local_backward, 0)

    def remote_backward(i, carry):
        weight = meta_ref[1, pl.ds(view_of_slot(i), 1), :]
        weight = jnp.where(i == 0, 0.0, weight)
        for p in range(PAIRS):
            cols = slice(p * 128, (p + 1) * 128)
            inner = slice((p % 2) * 128, (p % 2 + 1) * 128)
            _, ds = score_gradient(i, p)
            part = halves(tn(ds, kv_in[i, p // 2, 0, :, inner]))
            dq_acc[0:BLK, cols] += part * (1.0 - weight)
            dq_acc[BLK : 2 * BLK, cols] += part * weight
        return carry

    send_far(1, 2)
    lax.fori_loop(0, LOCAL, remote_backward, 0, unroll=4)
    dq_ref[...] = (dq_acc[...] * 0.125).astype(BF16)

    def owner_backward(half, j, n):
        i = slot_of(half, j, n)
        a, b = i // SIDE, i % SIDE
        if i == 0:
            weight = jnp.ones((1, 128), F32)
        elif b == 0:
            weight = meta_of("x", -a, 0, me)
        else:
            weight = block_in[b - 1, a : a + 1, :]
        weight16 = weight.astype(BF16)
        for p in (2 * half, 2 * half + 1):
            cols = slice(p * 128, (p + 1) * 128)
            inner = slice((p % 2) * 128, (p % 2 + 1) * 128)
            kp = pick(k_ref[0:BLK, cols], k_ref[BLK : 2 * BLK, cols], weight16)
            vp = pick(v_ref[0:BLK, cols], v_ref[BLK : 2 * BLK, cols], weight16)
            qp = stack(qg_in[i, half, 0, :, inner])
            gp = stack(qg_in[i, half, 1, :, inner])
            prob = jnp.exp(nt(kp, qp) - stat_in[i, p : p + 1, :])
            ds = (prob * (nt(vp, gp) - stat_in[i, 4 + p : 5 + p, :])).astype(BF16)
            dk = nn(ds, qp)
            dv = nn(prob.astype(BF16), gp)
            dk_acc[0:BLK, cols] += dk * (1.0 - weight)
            dk_acc[BLK : 2 * BLK, cols] += dk * weight
            dv_acc[0:BLK, cols] += dv * (1.0 - weight)
            dv_acc[BLK : 2 * BLK, cols] += dv * weight

    for c in (*blocks.values(), *stats.values()):
        c.wait_recv()
    for j in (0, 1, 3, 2):
        for n in (0, 1, 3, 2):
            wait_items(1, j, n)
            for half in range(2):
                owner_backward(half, j, n)

    dk_ref[...] = dk_acc[...].astype(BF16)
    dv_ref[...] = dv_acc[...].astype(BF16)
    for c in sent:
        c.wait_send()


def shards(queries, keys, values, out_grad, block_lists):
    vmem = pl.BlockSpec(memory_space=pltpu.VMEM)
    rows = 2 * BLK
    dma = pltpu.SemaphoreType.DMA
    stat_rows = (ENTRIES, PAIRS, HALF)
    return pl.pallas_call(
        kernel,
        out_shape=[pltpu.VMEM((rows, WIDTH), BF16)] * 3,
        in_specs=[pl.BlockSpec(memory_space=pl.ANY)] * 5,
        out_specs=[vmem] * 3,
        scratch_shapes=[
            pltpu.VMEM((2, 16), jnp.int32),
            *[pltpu.VMEM((rows, WIDTH), BF16)] * 5,
            pltpu.VMEM((3, 16, 128), F32),
            pltpu.VMEM((3, 2, 16, 128), F32),
            pltpu.VMEM((3, 2, 16, 128), F32),
            pltpu.VMEM((3, 8, 128), F32),
            pltpu.VMEM((3, 8, 128), F32),
            pltpu.VMEM((2, 2, 3, 2, rows, HALF), BF16),
            pltpu.VMEM((2, 2, 4, 3, 2, BLK, HALF), BF16),
            pltpu.VMEM((16, 2, 2, BLK, HALF), BF16),
            pltpu.VMEM((16, 2, 2, BLK, HALF), BF16),
            pltpu.VMEM((ENTRIES, PAIRS, BLK, HALF), F32),
            pltpu.VMEM((ENTRIES, PAIRS, BLK, HALF), F32),
            pltpu.VMEM(stat_rows, F32),
            pltpu.VMEM(stat_rows, F32),
            pltpu.VMEM(stat_rows, F32),
            pltpu.VMEM(stat_rows, F32),
            pltpu.VMEM((16, 8, HALF), F32),
            pltpu.VMEM((16, 8, HALF), F32),
            pltpu.VMEM((rows, WIDTH), F32),
            pltpu.VMEM((rows, WIDTH), F32),
            pltpu.VMEM((rows, WIDTH), F32),
            dma((2, 3)),
            dma((2, 3)),
            dma((2, 2, 4, 2)),
            dma((2, 2, 4, 2)),
            dma((2, 2, 4, 3)),
            dma((2, 2, 4, 3)),
            dma((2, 2, 2)),
            dma((2, 2, 2)),
            dma((16,)),
            dma((16,)),
            dma((5,)),
            dma((3,)),
            dma((3,)),
        ],
        compiler_params=pltpu.CompilerParams(
            collective_id=0, has_side_effects=True, vmem_limit_bytes=60 * 1024 * 1024
        ),
    )(block_lists, queries, keys, values, out_grad)


def solution(mesh):
    spec = P(("views", "sub"), None)
    return jax.shard_map(
        shards,
        mesh=mesh,
        in_specs=(spec,) * 5,
        out_specs=(spec,) * 3,
        check_vma=False,
    )
```

```python
import jax
import jax.numpy as jnp
from jax import lax
from jax.experimental import pallas as pl
from jax.experimental.pallas import tpu as pltpu
from jax.sharding import PartitionSpec as P

MESH = pl.DeviceIdType.MESH
F32 = jnp.float32
BF16 = jnp.bfloat16
SIDE = 4
BLK = 128
WIDTH = 512
HALF = 256
PAIRS = 4
LOCAL = 16
ENTRIES = 19
FAR = 1e30


def nt(a, b):
    return lax.dot_general(a, b, (((1,), (1,)), ((), ())), preferred_element_type=F32)


def nn(a, b):
    return lax.dot_general(a, b, (((1,), (0,)), ((), ())), preferred_element_type=F32)


def tn(a, b):
    return lax.dot_general(a, b, (((0,), (0,)), ((), ())), preferred_element_type=F32)


def pick(first, second, second_weight):
    return first * (1 - second_weight) + second * second_weight


def kernel(
    lists_hbm,
    q_hbm,
    k_hbm,
    v_hbm,
    g_hbm,
    out_ref,
    lists_ref,
    q_ref,
    k_ref,
    v_ref,
    g_ref,
    qs_ref,
    meta_ref,
    meta_x,
    meta_y,
    block_out,
    block_in,
    near,
    stage,
    kv_in,
    qg_in,
    raised_buf,
    grad_buf,
    max_buf,
    sum_buf,
    scale_buf,
    delta_buf,
    stat_out,
    stat_in,
    dq_acc,
    dk_acc,
    dv_acc,
    meta_ss,
    meta_rs,
    near_ss,
    near_rs,
    far_ss,
    far_rs,
    win_ss,
    win_rs,
    stat_ss,
    stat_rs,
    load_sem,
    block_ss,
    block_rs,
):
    loads = []
    for n, (src, dst) in enumerate(
        (
            (lists_hbm, lists_ref),
            (k_hbm, k_ref),
            (v_hbm, v_ref),
            (q_hbm, q_ref),
            (g_hbm, g_ref),
        )
    ):
        loads.append(pltpu.make_async_copy(src, dst, load_sem.at[n]))
        loads[n].start()
    me = lax.axis_index("views")
    band = lax.axis_index("sub")
    bands = lax.axis_size("sub")
    x, y = me // SIDE, me % SIDE
    after = lax.rem(band + 1, bands)
    ahead = lax.rem(band + bands - 1, bands)

    def view(a, b):
        return lax.rem(x + (a % SIDE), SIDE) * SIDE + lax.rem(y + (b % SIDE), SIDE)

    barrier = pltpu.get_barrier_semaphore()
    for d in (1, 3, 2):
        for peer in (view(d, 0), view(0, d)):
            pl.semaphore_signal(
                barrier, inc=1, device_id={"views": peer}, device_id_type=MESH
            )
    for s in (after, ahead):
        pl.semaphore_signal(barrier, inc=1, device_id={"sub": s}, device_id_type=MESH)

    loads[0].wait()
    lists = lists_ref[...]
    views = lax.broadcasted_iota(jnp.int32, (16, 16), 0)
    found = []
    for row in range(2):
        ids = jnp.broadcast_to(lists[row : row + 1, :], (16, 16))
        hit = (ids >= 0) & ((ids >> 4) == views)
        live = jnp.sum(jnp.where(hit, 1.0, 0.0), axis=1, keepdims=True)
        odd = jnp.sum(jnp.where(hit & ((ids & 1) == 1), 1.0, 0.0), axis=1, keepdims=True)
        found.append((live, odd))
    meta_ref[0] = jnp.broadcast_to(found[0][1] + found[1][1], (16, 128))
    meta_ref[1] = jnp.broadcast_to(found[1][0], (16, 128))
    meta_ref[2] = jnp.broadcast_to(found[0][0] + found[1][0], (16, 128))
    pl.semaphore_wait(barrier, 8)

    sent = []

    def copy(src, dst, ss, rs, **to):
        c = pltpu.make_async_remote_copy(
            src_ref=src,
            dst_ref=dst,
            send_sem=ss,
            recv_sem=rs,
            device_id=to,
            device_id_type=MESH,
        )
        c.start()
        sent.append(c)
        return c

    metas = {}
    for d in (1, 3, 2):
        metas["x", d] = copy(
            meta_ref.at[0:2],
            meta_x.at[d - 1],
            meta_ss.at[0, d - 1],
            meta_rs.at[0, d - 1],
            views=view(-d, 0),
        )
        metas["y", d] = copy(
            meta_ref.at[0:2],
            meta_y.at[d - 1],
            meta_ss.at[1, d - 1],
            meta_rs.at[1, d - 1],
            views=view(0, -d),
        )

    for c in loads[1:3]:
        c.wait()
    own = ((k_ref, v_ref), (qs_ref, g_ref))
    nears = {}

    def send_near(group):
        for arr in range(2):
            for d in (1, 3):
                for half in range(2):
                    nears[group, half, d, arr] = copy(
                        own[group][arr].at[:, half * HALF : (half + 1) * HALF],
                        near.at[group, half, d - 1, arr],
                        near_ss.at[group, half, d - 1, arr],
                        near_rs.at[group, half, d - 1, arr],
                        views=view(d, 0) if half == 0 else view(0, d),
                    )

    passed = {}

    def pass_on(group):
        for arr in range(2):
            for d in (1, 3):
                for half in range(2):
                    nears[group, half, d, arr].wait_recv()
                    rows = slice(0, BLK) if d == 1 else slice(BLK, 2 * BLK)
                    passed[group, half, d, arr] = copy(
                        near.at[group, half, d - 1, arr, rows, :],
                        near.at[group, half, 1, arr, rows, :],
                        near_ss.at[group, half, d, arr],
                        near_rs.at[group, half, d, arr],
                        views=view(d, 0) if half == 0 else view(0, d),
                    )

    wins = {}

    def send_window(group):
        rows = slice(BLK, 2 * BLK) if group == 0 else slice(0, BLK)
        target = kv_in if group == 0 else qg_in
        for arr in range(2):
            for half in range(2):
                wins[group, half, arr] = copy(
                    own[group][arr].at[rows, half * HALF : (half + 1) * HALF],
                    target.at[0, half, arr],
                    win_ss.at[group, half, arr],
                    win_rs.at[group, half, arr],
                    sub=after if group == 0 else ahead,
                )

    send_near(0)
    for c in loads[3:]:
        c.wait()
    qs_ref[...] = q_ref[...] * jnp.asarray(0.125, BF16)

    lane = lax.broadcasted_iota(jnp.int32, (1, 128), 1)
    low = jnp.where(lane < 64, 1.0, 0.0)
    low16, high16 = low.astype(BF16), (1.0 - low).astype(BF16)

    def stack(piece):
        return jnp.concatenate([piece * low16, piece * high16], axis=0)

    def wide(row):
        return jnp.concatenate([row, row], axis=1)

    def forward(entry, p, qp, gp, kp, vp):
        scores = nt(kp, stack(qp))
        grads = nt(vp, stack(gp))
        top = jnp.max(scores, axis=0, keepdims=True)
        raised = jnp.exp(scores - top)
        raised_buf[entry, p] = raised
        grad_buf[entry, p] = grads
        max_buf[entry, p : p + 1, :] = top
        sum_buf[entry, p : p + 1, :] = jnp.sum(raised, axis=0, keepdims=True)

    def local_forward(n, carry):
        q_rows = pl.ds(pl.multiple_of(jnp.minimum(n, 1) * BLK, BLK), BLK)
        k_rows = pl.ds(pl.multiple_of((n // 2) * BLK, BLK), BLK)
        for p in range(PAIRS):
            cols = slice(p * 128, (p + 1) * 128)
            forward(
                LOCAL + n,
                p,
                qs_ref[q_rows, cols],
                g_ref[q_rows, cols],
                k_ref[k_rows, cols],
                v_ref[k_rows, cols],
            )
        return carry

    for c in metas.values():
        c.wait_recv()

    def meta_of(axis, d, plane, row):
        if d % SIDE == 0:
            got = meta_ref[plane, pl.ds(row, 1), :]
        elif axis == "x":
            got = meta_x[d % SIDE - 1, plane, pl.ds(row, 1), :]
        else:
            got = meta_y[d % SIDE - 1, plane, pl.ds(row, 1), :]
        return got

    blocks = {}
    for d in (1, 3, 2):
        for a in range(SIDE):
            block_out[d - 1, a : a + 1, :] = meta_of("x", -a, 0, view(0, d))
        block_out[d - 1, 4:8, :] = jnp.zeros((4, 128), F32)
        blocks[d] = copy(
            block_out.at[d - 1],
            block_in.at[d - 1],
            block_ss.at[d - 1],
            block_rs.at[d - 1],
            views=view(0, d),
        )

    def want(group, half, j, d):
        if group == 0 and half == 0:
            return meta_of("y", d, 0, view(-j, 0))
        if group == 0:
            return meta_of("x", d, 0, view(0, -j))
        if half == 0:
            return meta_of("x", -j, 1, view(0, d))
        return meta_of("y", -j, 1, view(d, 0))

    fars = {}

    def send_far(group, j):
        if j == 2:
            for c in (passed[group, h, d, r] for h in range(2) for d in (1, 3) for r in range(2)):
                c.wait_recv()
        target = kv_in if group == 0 else qg_in
        for d in (1, 3, 2, 0):
            for half in range(2):
                if d == 0 and j == 0:
                    continue
                slot = j * SIDE + d if half == 0 else d * SIDE + j
                weight = wide(want(group, half, j, d).astype(BF16))
                for arr in range(2):
                    if j:
                        first = near[group, half, j - 1, arr, 0:BLK, :]
                        second = near[group, half, j - 1, arr, BLK : 2 * BLK, :]
                    else:
                        cols = slice(half * HALF, (half + 1) * HALF)
                        first = own[group][arr][0:BLK, cols]
                        second = own[group][arr][BLK : 2 * BLK, cols]
                    chosen = pick(first, second, weight)
                    if d:
                        stage[group, half, j, d - 1, arr] = chosen
                    else:
                        target[slot, half, arr] = chosen
                if d:
                    fars[group, half, slot] = copy(
                        stage.at[group, half, j, d - 1],
                        target.at[slot, half],
                        far_ss.at[group, half, j, d - 1],
                        far_rs.at[group, half, j, d - 1],
                        views=view(0, d) if half == 0 else view(d, 0),
                    )

    send_far(0, 0)
    send_window(0)
    send_window(1)
    lax.fori_loop(0, 3, local_forward, 0, unroll=3)
    pass_on(0)
    send_far(0, 1)
    send_far(0, 3)
    send_far(0, 2)
    send_near(1)

    def view_of_slot(i):
        return lax.rem(x + SIDE - i // SIDE, SIDE) * SIDE + lax.rem(y + SIDE - i % SIDE, SIDE)

    def slot_of(half, j, n):
        return j * SIDE + n if half == 0 else n * SIDE + j

    def remote_forward(half, j, n):
        i = slot_of(half, j, n)
        weight = meta_ref[1, pl.ds(view_of_slot(i), 1), :].astype(BF16)
        if i == 0:
            weight = weight * 0
        for p in (2 * half, 2 * half + 1):
            cols = slice(p * 128, (p + 1) * 128)
            inner = slice((p % 2) * 128, (p % 2 + 1) * 128)
            forward(
                i,
                p,
                pick(qs_ref[0:BLK, cols], qs_ref[BLK : 2 * BLK, cols], weight),
                pick(g_ref[0:BLK, cols], g_ref[BLK : 2 * BLK, cols], weight),
                kv_in[i, half, 0, :, inner],
                kv_in[i, half, 1, :, inner],
            )

    def wait_items(group, j, n):
        for half in range(2):
            if n:
                fars[group, half, slot_of(half, j, n)].wait_recv()
            elif j == 0:
                for arr in range(2):
                    wins[group, half, arr].wait_recv()

    for j in (0, 1, 3, 2):
        for n in (0, 1, 3, 2):
            wait_items(0, j, n)
            for half in range(2):
                remote_forward(half, j, n)
        if j == 1:
            send_far(1, 0)

    has_prev = jnp.where(band > 0, 1.0, 0.0)
    ones = jnp.full((1, HALF), 1.0, F32)
    uses = []
    for e in range(ENTRIES):
        if e == 0:
            uses.append((ones * has_prev, ones * 0.0))
        elif e < LOCAL:
            row = view(-(e // SIDE), -(e % SIDE))
            second = wide(meta_ref[1, pl.ds(row, 1), :])
            live = wide(meta_ref[2, pl.ds(row, 1), :])
            uses.append((live * (1.0 - second), live * second))
        else:
            second = ones * (0.0 if e == LOCAL else 1.0)
            uses.append((1.0 - second, second))
    tops, invs = [], []
    for blk in range(2):
        top = jnp.full((PAIRS, HALF), -FAR, F32)
        for e in range(ENTRIES):
            top = jnp.maximum(top, max_buf[e] + (uses[e][blk] - 1.0) * FAR)
        tops.append(top)
        total = jnp.zeros((PAIRS, HALF), F32)
        for e in range(ENTRIES):
            total += uses[e][blk] * sum_buf[e] * jnp.exp(jnp.minimum(max_buf[e] - top, 0.0))
        invs.append(1.0 / total)
    for e in range(ENTRIES):
        scale_buf[e] = sum(
            uses[e][blk] * jnp.exp(jnp.minimum(max_buf[e] - tops[blk], 0.0)) * invs[blk]
            for blk in range(2)
        )

    def delta_part(e, carry):
        for p in range(PAIRS):
            prob = raised_buf[e, p] * scale_buf[e, p : p + 1, :]
            rounded = prob.astype(BF16).astype(F32)
            delta_buf[e, p : p + 1, :] = jnp.sum(rounded * grad_buf[e, p], axis=0, keepdims=True)
        return carry

    lax.fori_loop(0, LOCAL, delta_part, 0, unroll=4)
    lax.fori_loop(LOCAL, ENTRIES, delta_part, 0, unroll=3)
    deltas = [
        sum(uses[e][blk] * delta_buf[e] for e in range(ENTRIES)) for blk in range(2)
    ]
    logs = [tops[blk] - jnp.log(invs[blk]) for blk in range(2)]
    stats = {}
    for e in range(ENTRIES):
        first, second = uses[e]
        delta = first * deltas[0] + second * deltas[1]
        delta_buf[e] = delta
        if e < LOCAL:
            a, b = e // SIDE, e % SIDE
            stat_out[e, 0:4, :] = first * logs[0] + second * logs[1] + (1.0 - first - second) * FAR
            stat_out[e, 4:8, :] = delta
            slot = (-a % SIDE) * SIDE + (-b % SIDE)
            to = {"views": view(-a, -b)} if e else {"sub": ahead}
            stats[slot] = copy(
                stat_out.at[e], stat_in.at[slot], stat_ss.at[slot], stat_rs.at[slot], **to
            )

    pass_on(1)
    send_far(1, 1)
    send_far(1, 3)

    dq_acc[...] = jnp.zeros_like(dq_acc)
    dk_acc[...] = jnp.zeros_like(dk_acc)
    dv_acc[...] = jnp.zeros_like(dv_acc)

    def score_gradient(e, p):
        prob = raised_buf[e, p] * scale_buf[e, p : p + 1, :]
        return prob, (prob * (grad_buf[e, p] - delta_buf[e, p : p + 1, :])).astype(BF16)

    def halves(both):
        return jnp.where(lane < 64, both[0:BLK, :], both[BLK : 2 * BLK, :])

    def local_backward(n, carry):
        q_rows = pl.ds(pl.multiple_of(jnp.minimum(n, 1) * BLK, BLK), BLK)
        k_rows = pl.ds(pl.multiple_of((n // 2) * BLK, BLK), BLK)
        for p in range(PAIRS):
            cols = slice(p * 128, (p + 1) * 128)
            prob, ds = score_gradient(LOCAL + n, p)
            dq_acc[q_rows, cols] += halves(tn(ds, k_ref[k_rows, cols]))
            dk_acc[k_rows, cols] += nn(ds, stack(qs_ref[q_rows, cols]))
            dv_acc[k_rows, cols] += nn(prob.astype(BF16), stack(g_ref[q_rows, cols]))
        return carry

    lax.fori_loop(0, 3, local_backward, 0, unroll=3)

    def remote_backward(i, carry):
        weight = meta_ref[1, pl.ds(view_of_slot(i), 1), :]
        weight = jnp.where(i == 0, 0.0, weight)
        for p in range(PAIRS):
            cols = slice(p * 128, (p + 1) * 128)
            inner = slice((p % 2) * 128, (p % 2 + 1) * 128)
            _, ds = score_gradient(i, p)
            part = halves(tn(ds, kv_in[i, p // 2, 0, :, inner]))
            dq_acc[0:BLK, cols] += part * (1.0 - weight)
            dq_acc[BLK : 2 * BLK, cols] += part * weight
        return carry

    send_far(1, 2)
    lax.fori_loop(0, LOCAL, remote_backward, 0, unroll=4)
    out_ref[0] = (dq_acc[...] * 0.125).astype(BF16)

    def owner_backward(half, j, n):
        i = slot_of(half, j, n)
        a, b = i // SIDE, i % SIDE
        if i == 0:
            weight = jnp.ones((1, 128), F32)
        elif b == 0:
            weight = meta_of("x", -a, 0, me)
        else:
            weight = block_in[b - 1, a : a + 1, :]
        weight16 = weight.astype(BF16)
        for p in (2 * half, 2 * half + 1):
            cols = slice(p * 128, (p + 1) * 128)
            inner = slice((p % 2) * 128, (p % 2 + 1) * 128)
            kp = pick(k_ref[0:BLK, cols], k_ref[BLK : 2 * BLK, cols], weight16)
            vp = pick(v_ref[0:BLK, cols], v_ref[BLK : 2 * BLK, cols], weight16)
            qp = stack(qg_in[i, half, 0, :, inner])
            gp = stack(qg_in[i, half, 1, :, inner])
            prob = jnp.exp(nt(kp, qp) - stat_in[i, p : p + 1, :])
            ds = (prob * (nt(vp, gp) - stat_in[i, 4 + p : 5 + p, :])).astype(BF16)
            dk = nn(ds, qp)
            dv = nn(prob.astype(BF16), gp)
            dk_acc[0:BLK, cols] += dk * (1.0 - weight)
            dk_acc[BLK : 2 * BLK, cols] += dk * weight
            dv_acc[0:BLK, cols] += dv * (1.0 - weight)
            dv_acc[BLK : 2 * BLK, cols] += dv * weight

    for c in (*blocks.values(), *stats.values()):
        c.wait_recv()
    for j in (0, 1, 3, 2):
        for n in (0, 1, 3, 2):
            wait_items(1, j, n)
            for half in range(2):
                owner_backward(half, j, n)

    out_ref[1] = dk_acc[...].astype(BF16)
    out_ref[2] = dv_acc[...].astype(BF16)
    for c in sent:
        c.wait_send()


def shards(queries, keys, values, out_grad, block_lists):
    vmem = pl.BlockSpec(memory_space=pltpu.VMEM)
    rows = 2 * BLK
    dma = pltpu.SemaphoreType.DMA
    stat_rows = (ENTRIES, PAIRS, HALF)
    out = pl.pallas_call(
        kernel,
        out_shape=pltpu.VMEM((3, rows, WIDTH), BF16),
        in_specs=[pl.BlockSpec(memory_space=pl.ANY)] * 5,
        out_specs=vmem,
        scratch_shapes=[
            pltpu.VMEM((2, 16), jnp.int32),
            *[pltpu.VMEM((rows, WIDTH), BF16)] * 5,
            pltpu.VMEM((3, 16, 128), F32),
            pltpu.VMEM((3, 2, 16, 128), F32),
            pltpu.VMEM((3, 2, 16, 128), F32),
            pltpu.VMEM((3, 8, 128), F32),
            pltpu.VMEM((3, 8, 128), F32),
            pltpu.VMEM((2, 2, 3, 2, rows, HALF), BF16),
            pltpu.VMEM((2, 2, 4, 3, 2, BLK, HALF), BF16),
            pltpu.VMEM((16, 2, 2, BLK, HALF), BF16),
            pltpu.VMEM((16, 2, 2, BLK, HALF), BF16),
            pltpu.VMEM((ENTRIES, PAIRS, BLK, HALF), F32),
            pltpu.VMEM((ENTRIES, PAIRS, BLK, HALF), F32),
            pltpu.VMEM(stat_rows, F32),
            pltpu.VMEM(stat_rows, F32),
            pltpu.VMEM(stat_rows, F32),
            pltpu.VMEM(stat_rows, F32),
            pltpu.VMEM((16, 8, HALF), F32),
            pltpu.VMEM((16, 8, HALF), F32),
            pltpu.VMEM((rows, WIDTH), F32),
            pltpu.VMEM((rows, WIDTH), F32),
            pltpu.VMEM((rows, WIDTH), F32),
            dma((2, 3)),
            dma((2, 3)),
            dma((2, 2, 4, 2)),
            dma((2, 2, 4, 2)),
            dma((2, 2, 4, 3)),
            dma((2, 2, 4, 3)),
            dma((2, 2, 2)),
            dma((2, 2, 2)),
            dma((16,)),
            dma((16,)),
            dma((5,)),
            dma((3,)),
            dma((3,)),
        ],
        compiler_params=pltpu.CompilerParams(
            collective_id=0, has_side_effects=True, vmem_limit_bytes=60 * 1024 * 1024
        ),
    )(block_lists, queries, keys, values, out_grad)
    return out[0], out[1], out[2]


def solution(mesh):
    spec = P(("views", "sub"), None)
    return jax.shard_map(
        shards,
        mesh=mesh,
        in_specs=(spec,) * 5,
        out_specs=(spec,) * 3,
        check_vma=False,
    )
```

```python
import jax
import jax.numpy as jnp
from jax import lax
from jax.experimental import pallas as pl
from jax.experimental.pallas import tpu as pltpu
from jax.sharding import PartitionSpec as P

MESH = pl.DeviceIdType.MESH
F32 = jnp.float32
BF16 = jnp.bfloat16
SIDE = 4
BLK = 128
WIDTH = 512
HALF = 256
PAIRS = 4
LOCAL = 16
ENTRIES = 19
FAR = 1e30


def nt(a, b):
    return lax.dot_general(a, b, (((1,), (1,)), ((), ())), preferred_element_type=F32)


def nn(a, b):
    return lax.dot_general(a, b, (((1,), (0,)), ((), ())), preferred_element_type=F32)


def tn(a, b):
    return lax.dot_general(a, b, (((0,), (0,)), ((), ())), preferred_element_type=F32)


def pick(first, second, second_weight):
    return first * (1 - second_weight) + second * second_weight


def kernel(
    lists_hbm,
    q_hbm,
    k_hbm,
    v_hbm,
    g_hbm,
    out_ref,
    lists_ref,
    q_ref,
    k_ref,
    v_ref,
    g_ref,
    qs_ref,
    meta_ref,
    meta_x,
    meta_y,
    block_out,
    block_in,
    near,
    stage,
    kv_in,
    qg_in,
    raised_buf,
    grad_buf,
    max_buf,
    sum_buf,
    scale_buf,
    delta_buf,
    stat_out,
    stat_in,
    dq_acc,
    dk_acc,
    dv_acc,
    meta_ss,
    meta_rs,
    near_ss,
    near_rs,
    far_ss,
    far_rs,
    win_ss,
    win_rs,
    stat_ss,
    stat_rs,
    load_sem,
    block_ss,
    block_rs,
):
    loads = []
    for n, (src, dst) in enumerate(
        (
            (lists_hbm, lists_ref),
            (k_hbm, k_ref),
            (v_hbm, v_ref),
            (q_hbm, q_ref),
            (g_hbm, g_ref),
        )
    ):
        loads.append(pltpu.make_async_copy(src, dst, load_sem.at[n]))
        loads[n].start()
    me = lax.axis_index("views")
    band = lax.axis_index("sub")
    bands = lax.axis_size("sub")
    x, y = me // SIDE, me % SIDE
    after = lax.rem(band + 1, bands)
    ahead = lax.rem(band + bands - 1, bands)

    def view(a, b):
        return lax.rem(x + (a % SIDE), SIDE) * SIDE + lax.rem(y + (b % SIDE), SIDE)

    barrier = pltpu.get_barrier_semaphore()
    for d in (1, 3, 2):
        for peer in (view(d, 0), view(0, d)):
            pl.semaphore_signal(
                barrier, inc=1, device_id={"views": peer}, device_id_type=MESH
            )
    for s in (after, ahead):
        pl.semaphore_signal(barrier, inc=1, device_id={"sub": s}, device_id_type=MESH)

    loads[0].wait()
    lists = lists_ref[...]
    views = lax.broadcasted_iota(jnp.int32, (16, 16), 0)
    found = []
    for row in range(2):
        ids = jnp.broadcast_to(lists[row : row + 1, :], (16, 16))
        hit = (ids >= 0) & ((ids >> 4) == views)
        live = jnp.sum(jnp.where(hit, 1.0, 0.0), axis=1, keepdims=True)
        odd = jnp.sum(jnp.where(hit & ((ids & 1) == 1), 1.0, 0.0), axis=1, keepdims=True)
        found.append((live, odd))
    meta_ref[0] = jnp.broadcast_to(found[0][1] + found[1][1], (16, 128))
    meta_ref[1] = jnp.broadcast_to(found[1][0], (16, 128))
    meta_ref[2] = jnp.broadcast_to(found[0][0] + found[1][0], (16, 128))
    pl.semaphore_wait(barrier, 8)

    sent = []

    def copy(src, dst, ss, rs, **to):
        c = pltpu.make_async_remote_copy(
            src_ref=src,
            dst_ref=dst,
            send_sem=ss,
            recv_sem=rs,
            device_id=to,
            device_id_type=MESH,
        )
        c.start()
        sent.append(c)
        return c

    metas = {}
    for d in (1, 3, 2):
        metas["x", d] = copy(
            meta_ref.at[0:2],
            meta_x.at[d - 1],
            meta_ss.at[0, d - 1],
            meta_rs.at[0, d - 1],
            views=view(-d, 0),
        )
        metas["y", d] = copy(
            meta_ref.at[0:2],
            meta_y.at[d - 1],
            meta_ss.at[1, d - 1],
            meta_rs.at[1, d - 1],
            views=view(0, -d),
        )

    for c in loads[1:3]:
        c.wait()
    own = ((k_ref, v_ref), (qs_ref, g_ref))
    nears = {}

    def send_near(group):
        for arr in range(2):
            for d in (1, 3):
                for half in range(2):
                    nears[group, half, d, arr] = copy(
                        own[group][arr].at[:, half * HALF : (half + 1) * HALF],
                        near.at[group, half, d - 1, arr],
                        near_ss.at[group, half, d - 1, arr],
                        near_rs.at[group, half, d - 1, arr],
                        views=view(d, 0) if half == 0 else view(0, d),
                    )

    passed = {}

    def pass_on(group):
        for arr in range(2):
            for d in (1, 3):
                for half in range(2):
                    nears[group, half, d, arr].wait_recv()
                    rows = slice(0, BLK) if d == 1 else slice(BLK, 2 * BLK)
                    passed[group, half, d, arr] = copy(
                        near.at[group, half, d - 1, arr, rows, :],
                        near.at[group, half, 1, arr, rows, :],
                        near_ss.at[group, half, d, arr],
                        near_rs.at[group, half, d, arr],
                        views=view(d, 0) if half == 0 else view(0, d),
                    )

    wins = {}

    def send_window(group):
        rows = slice(BLK, 2 * BLK) if group == 0 else slice(0, BLK)
        target = kv_in if group == 0 else qg_in
        for arr in range(2):
            for half in range(2):
                wins[group, half, arr] = copy(
                    own[group][arr].at[rows, half * HALF : (half + 1) * HALF],
                    target.at[0, half, arr],
                    win_ss.at[group, half, arr],
                    win_rs.at[group, half, arr],
                    sub=after if group == 0 else ahead,
                )

    send_near(0)
    for c in loads[3:]:
        c.wait()
    qs_ref[...] = q_ref[...] * jnp.asarray(0.125, BF16)

    lane = lax.broadcasted_iota(jnp.int32, (1, 128), 1)
    low = jnp.where(lane < 64, 1.0, 0.0)
    low16, high16 = low.astype(BF16), (1.0 - low).astype(BF16)

    def stack(piece):
        return jnp.concatenate([piece * low16, piece * high16], axis=0)

    def wide(row):
        return jnp.concatenate([row, row], axis=1)

    def forward(entry, p, qp, gp, kp, vp):
        scores = nt(kp, stack(qp))
        grads = nt(vp, stack(gp))
        top = jnp.max(scores, axis=0, keepdims=True)
        raised = jnp.exp(scores - top)
        raised_buf[entry, p] = raised
        grad_buf[entry, p] = grads
        max_buf[entry, p : p + 1, :] = top
        sum_buf[entry, p : p + 1, :] = jnp.sum(raised, axis=0, keepdims=True)

    def local_forward(n, carry):
        q_rows = pl.ds(pl.multiple_of(jnp.minimum(n, 1) * BLK, BLK), BLK)
        k_rows = pl.ds(pl.multiple_of((n // 2) * BLK, BLK), BLK)
        for p in range(PAIRS):
            cols = slice(p * 128, (p + 1) * 128)
            forward(
                LOCAL + n,
                p,
                qs_ref[q_rows, cols],
                g_ref[q_rows, cols],
                k_ref[k_rows, cols],
                v_ref[k_rows, cols],
            )
        return carry

    for c in metas.values():
        c.wait_recv()

    def meta_of(axis, d, plane, row):
        if d % SIDE == 0:
            got = meta_ref[plane, pl.ds(row, 1), :]
        elif axis == "x":
            got = meta_x[d % SIDE - 1, plane, pl.ds(row, 1), :]
        else:
            got = meta_y[d % SIDE - 1, plane, pl.ds(row, 1), :]
        return got

    def want(group, half, j, d):
        if group == 0 and half == 0:
            return meta_of("y", d, 0, view(-j, 0))
        if group == 0:
            return meta_of("x", d, 0, view(0, -j))
        if half == 0:
            return meta_of("x", -j, 1, view(0, d))
        return meta_of("y", -j, 1, view(d, 0))

    fars = {}

    def send_far(group, j):
        if j == 2:
            for c in (passed[group, h, d, r] for h in range(2) for d in (1, 3) for r in range(2)):
                c.wait_recv()
        target = kv_in if group == 0 else qg_in
        for d in (1, 3, 2, 0):
            for half in range(2):
                if d == 0 and j == 0:
                    continue
                slot = j * SIDE + d if half == 0 else d * SIDE + j
                weight = wide(want(group, half, j, d).astype(BF16))
                for arr in range(2):
                    if j:
                        first = near[group, half, j - 1, arr, 0:BLK, :]
                        second = near[group, half, j - 1, arr, BLK : 2 * BLK, :]
                    else:
                        cols = slice(half * HALF, (half + 1) * HALF)
                        first = own[group][arr][0:BLK, cols]
                        second = own[group][arr][BLK : 2 * BLK, cols]
                    chosen = pick(first, second, weight)
                    if d:
                        stage[group, half, j, d - 1, arr] = chosen
                    else:
                        target[slot, half, arr] = chosen
                if d:
                    fars[group, half, slot] = copy(
                        stage.at[group, half, j, d - 1],
                        target.at[slot, half],
                        far_ss.at[group, half, j, d - 1],
                        far_rs.at[group, half, j, d - 1],
                        views=view(0, d) if half == 0 else view(d, 0),
                    )

    send_far(0, 0)
    send_window(0)
    send_window(1)
    lax.fori_loop(0, 3, local_forward, 0, unroll=3)
    pass_on(0)
    send_far(0, 1)
    send_far(0, 3)
    send_far(0, 2)
    send_near(1)
    blocks = {}
    for d in (1, 3, 2):
        for a in range(SIDE):
            block_out[d - 1, a : a + 1, :] = meta_of("x", -a, 0, view(0, d))
        block_out[d - 1, 4:8, :] = jnp.zeros((4, 128), F32)
        blocks[d] = copy(
            block_out.at[d - 1],
            block_in.at[d - 1],
            block_ss.at[d - 1],
            block_rs.at[d - 1],
            views=view(0, d),
        )

    def view_of_slot(i):
        return lax.rem(x + SIDE - i // SIDE, SIDE) * SIDE + lax.rem(y + SIDE - i % SIDE, SIDE)

    def slot_of(half, j, n):
        return j * SIDE + n if half == 0 else n * SIDE + j

    def remote_forward(half, j, n):
        i = slot_of(half, j, n)
        weight = meta_ref[1, pl.ds(view_of_slot(i), 1), :].astype(BF16)
        if i == 0:
            weight = weight * 0
        for p in (2 * half, 2 * half + 1):
            cols = slice(p * 128, (p + 1) * 128)
            inner = slice((p % 2) * 128, (p % 2 + 1) * 128)
            forward(
                i,
                p,
                pick(qs_ref[0:BLK, cols], qs_ref[BLK : 2 * BLK, cols], weight),
                pick(g_ref[0:BLK, cols], g_ref[BLK : 2 * BLK, cols], weight),
                kv_in[i, half, 0, :, inner],
                kv_in[i, half, 1, :, inner],
            )

    def wait_items(group, j, n):
        for half in range(2):
            if n:
                fars[group, half, slot_of(half, j, n)].wait_recv()
            elif j == 0:
                for arr in range(2):
                    wins[group, half, arr].wait_recv()

    for j in (0, 1, 3, 2):
        for n in (0, 1, 3, 2):
            wait_items(0, j, n)
            for half in range(2):
                remote_forward(half, j, n)
        if j == 1:
            send_far(1, 0)

    pass_on(1)

    has_prev = jnp.where(band > 0, 1.0, 0.0)
    ones = jnp.full((1, HALF), 1.0, F32)
    uses = []
    for e in range(ENTRIES):
        if e == 0:
            uses.append((ones * has_prev, ones * 0.0))
        elif e < LOCAL:
            row = view(-(e // SIDE), -(e % SIDE))
            second = wide(meta_ref[1, pl.ds(row, 1), :])
            live = wide(meta_ref[2, pl.ds(row, 1), :])
            uses.append((live * (1.0 - second), live * second))
        else:
            second = ones * (0.0 if e == LOCAL else 1.0)
            uses.append((1.0 - second, second))
    tops, invs = [], []
    for blk in range(2):
        top = jnp.full((PAIRS, HALF), -FAR, F32)
        for e in range(ENTRIES):
            top = jnp.maximum(top, max_buf[e] + (uses[e][blk] - 1.0) * FAR)
        tops.append(top)
        total = jnp.zeros((PAIRS, HALF), F32)
        for e in range(ENTRIES):
            total += uses[e][blk] * sum_buf[e] * jnp.exp(jnp.minimum(max_buf[e] - top, 0.0))
        invs.append(1.0 / total)
    for e in range(ENTRIES):
        scale_buf[e] = sum(
            uses[e][blk] * jnp.exp(jnp.minimum(max_buf[e] - tops[blk], 0.0)) * invs[blk]
            for blk in range(2)
        )

    def delta_part(e, carry):
        for p in range(PAIRS):
            prob = raised_buf[e, p] * scale_buf[e, p : p + 1, :]
            rounded = prob.astype(BF16).astype(F32)
            delta_buf[e, p : p + 1, :] = jnp.sum(rounded * grad_buf[e, p], axis=0, keepdims=True)
        return carry

    lax.fori_loop(0, LOCAL, delta_part, 0, unroll=4)
    lax.fori_loop(LOCAL, ENTRIES, delta_part, 0, unroll=3)
    deltas = [
        sum(uses[e][blk] * delta_buf[e] for e in range(ENTRIES)) for blk in range(2)
    ]
    logs = [tops[blk] - jnp.log(invs[blk]) for blk in range(2)]
    stats = {}
    for e in range(ENTRIES):
        first, second = uses[e]
        delta = first * deltas[0] + second * deltas[1]
        delta_buf[e] = delta
        if e < LOCAL:
            a, b = e // SIDE, e % SIDE
            stat_out[e, 0:4, :] = first * logs[0] + second * logs[1] + (1.0 - first - second) * FAR
            stat_out[e, 4:8, :] = delta
            slot = (-a % SIDE) * SIDE + (-b % SIDE)
            to = {"views": view(-a, -b)} if e else {"sub": ahead}
            stats[slot] = copy(
                stat_out.at[e], stat_in.at[slot], stat_ss.at[slot], stat_rs.at[slot], **to
            )

    send_far(1, 1)
    send_far(1, 3)

    dq_acc[...] = jnp.zeros_like(dq_acc)
    dk_acc[...] = jnp.zeros_like(dk_acc)
    dv_acc[...] = jnp.zeros_like(dv_acc)

    def score_gradient(e, p):
        prob = raised_buf[e, p] * scale_buf[e, p : p + 1, :]
        return prob, (prob * (grad_buf[e, p] - delta_buf[e, p : p + 1, :])).astype(BF16)

    def halves(both):
        return jnp.where(lane < 64, both[0:BLK, :], both[BLK : 2 * BLK, :])

    def local_backward(n, carry):
        q_rows = pl.ds(pl.multiple_of(jnp.minimum(n, 1) * BLK, BLK), BLK)
        k_rows = pl.ds(pl.multiple_of((n // 2) * BLK, BLK), BLK)
        for p in range(PAIRS):
            cols = slice(p * 128, (p + 1) * 128)
            prob, ds = score_gradient(LOCAL + n, p)
            dq_acc[q_rows, cols] += halves(tn(ds, k_ref[k_rows, cols]))
            dk_acc[k_rows, cols] += nn(ds, stack(qs_ref[q_rows, cols]))
            dv_acc[k_rows, cols] += nn(prob.astype(BF16), stack(g_ref[q_rows, cols]))
        return carry

    lax.fori_loop(0, 3, local_backward, 0, unroll=3)

    def remote_backward(i, carry):
        weight = meta_ref[1, pl.ds(view_of_slot(i), 1), :]
        weight = jnp.where(i == 0, 0.0, weight)
        for p in range(PAIRS):
            cols = slice(p * 128, (p + 1) * 128)
            inner = slice((p % 2) * 128, (p % 2 + 1) * 128)
            _, ds = score_gradient(i, p)
            part = halves(tn(ds, kv_in[i, p // 2, 0, :, inner]))
            dq_acc[0:BLK, cols] += part * (1.0 - weight)
            dq_acc[BLK : 2 * BLK, cols] += part * weight
        return carry

    send_far(1, 2)
    lax.fori_loop(0, LOCAL, remote_backward, 0, unroll=4)
    out_ref[0] = (dq_acc[...] * 0.125).astype(BF16)

    def owner_backward(half, j, n):
        i = slot_of(half, j, n)
        a, b = i // SIDE, i % SIDE
        if i == 0:
            weight = jnp.ones((1, 128), F32)
        elif b == 0:
            weight = meta_of("x", -a, 0, me)
        else:
            weight = block_in[b - 1, a : a + 1, :]
        weight16 = weight.astype(BF16)
        for p in (2 * half, 2 * half + 1):
            cols = slice(p * 128, (p + 1) * 128)
            inner = slice((p % 2) * 128, (p % 2 + 1) * 128)
            kp = pick(k_ref[0:BLK, cols], k_ref[BLK : 2 * BLK, cols], weight16)
            vp = pick(v_ref[0:BLK, cols], v_ref[BLK : 2 * BLK, cols], weight16)
            qp = stack(qg_in[i, half, 0, :, inner])
            gp = stack(qg_in[i, half, 1, :, inner])
            prob = jnp.exp(nt(kp, qp) - stat_in[i, p : p + 1, :])
            ds = (prob * (nt(vp, gp) - stat_in[i, 4 + p : 5 + p, :])).astype(BF16)
            dk = nn(ds, qp)
            dv = nn(prob.astype(BF16), gp)
            dk_acc[0:BLK, cols] += dk * (1.0 - weight)
            dk_acc[BLK : 2 * BLK, cols] += dk * weight
            dv_acc[0:BLK, cols] += dv * (1.0 - weight)
            dv_acc[BLK : 2 * BLK, cols] += dv * weight

    for c in (*blocks.values(), *stats.values()):
        c.wait_recv()
    for j in (0, 1, 3, 2):
        for n in (0, 1, 3, 2):
            wait_items(1, j, n)
            for half in range(2):
                owner_backward(half, j, n)

    out_ref[1] = dk_acc[...].astype(BF16)
    out_ref[2] = dv_acc[...].astype(BF16)
    for c in sent:
        c.wait_send()


def shards(queries, keys, values, out_grad, block_lists):
    vmem = pl.BlockSpec(memory_space=pltpu.VMEM)
    rows = 2 * BLK
    dma = pltpu.SemaphoreType.DMA
    stat_rows = (ENTRIES, PAIRS, HALF)
    out = pl.pallas_call(
        kernel,
        out_shape=pltpu.VMEM((3, rows, WIDTH), BF16),
        in_specs=[pl.BlockSpec(memory_space=pl.ANY)] * 5,
        out_specs=vmem,
        scratch_shapes=[
            pltpu.VMEM((2, 16), jnp.int32),
            *[pltpu.VMEM((rows, WIDTH), BF16)] * 5,
            pltpu.VMEM((3, 16, 128), F32),
            pltpu.VMEM((3, 2, 16, 128), F32),
            pltpu.VMEM((3, 2, 16, 128), F32),
            pltpu.VMEM((3, 8, 128), F32),
            pltpu.VMEM((3, 8, 128), F32),
            pltpu.VMEM((2, 2, 3, 2, rows, HALF), BF16),
            pltpu.VMEM((2, 2, 4, 3, 2, BLK, HALF), BF16),
            pltpu.VMEM((16, 2, 2, BLK, HALF), BF16),
            pltpu.VMEM((16, 2, 2, BLK, HALF), BF16),
            pltpu.VMEM((ENTRIES, PAIRS, BLK, HALF), F32),
            pltpu.VMEM((ENTRIES, PAIRS, BLK, HALF), F32),
            pltpu.VMEM(stat_rows, F32),
            pltpu.VMEM(stat_rows, F32),
            pltpu.VMEM(stat_rows, F32),
            pltpu.VMEM(stat_rows, F32),
            pltpu.VMEM((16, 8, HALF), F32),
            pltpu.VMEM((16, 8, HALF), F32),
            pltpu.VMEM((rows, WIDTH), F32),
            pltpu.VMEM((rows, WIDTH), F32),
            pltpu.VMEM((rows, WIDTH), F32),
            dma((2, 3)),
            dma((2, 3)),
            dma((2, 2, 4, 2)),
            dma((2, 2, 4, 2)),
            dma((2, 2, 4, 3)),
            dma((2, 2, 4, 3)),
            dma((2, 2, 2)),
            dma((2, 2, 2)),
            dma((16,)),
            dma((16,)),
            dma((5,)),
            dma((3,)),
            dma((3,)),
        ],
        compiler_params=pltpu.CompilerParams(
            collective_id=0, has_side_effects=True, vmem_limit_bytes=60 * 1024 * 1024
        ),
    )(block_lists, queries, keys, values, out_grad)
    return out[0], out[1], out[2]


def solution(mesh):
    spec = P(("views", "sub"), None)
    return jax.shard_map(
        shards,
        mesh=mesh,
        in_specs=(spec,) * 5,
        out_specs=(spec,) * 3,
        check_vma=False,
    )
```
